512 devices in a mesh: rep: 16 (over x_lo, z), fsdp: 32 (over y, x_hi, core).
Axes of the slice: x: 4 (x_hi: 2, x_lo: 2; x = x_hi * 2 + x_lo), y: 8, z: 8, core: 2. Of those that a mesh axis runs over, the one named last changes fastest.
Arguments:
- hid_acts: bfloat16 [1, 98304, 448], P(None, ('rep', 'fsdp')), may hold values from -16 to 16
- out_cot: bfloat16 [1, 98304, 4608], P(None, ('rep', 'fsdp')), may hold values from -6 to 6
- momentum: float32 [16, 448, 1, 4608], P('rep', 'fsdp'), may hold values from -6 to 6
- weight: bfloat16 [448, 1, 4608], P('fsdp'), may hold values from -0.25 to 0.25
- next_acts: bfloat16 [1, 98304, 448], P(None, ('rep', 'fsdp')), may hold values from -6 to 6
Outputs:
- next_out: bfloat16 [1, 98304, 4608], P(None, ('rep', 'fsdp'))
- new_momentum: float32 [16, 448, 1, 4608], P('rep', 'fsdp')
The draws below stay inside these ranges and needn't reach their ends.
All inputs are finite; a program needn't handle non-finite values.
Results may differ from the reference program's by a relative error of at most 0.02.
Values may be sent and summed in bfloat16 or wider, within the bound.
A program may use at most 128 MiB of HBM per device.

```python
import math
import jax
import jax.numpy as jnp
from jax import lax

D = 4608
TOK_DEV = 192
LAYERS = 1
SPAN = 256
KEEP = 32
ROWS = 448
TOKENS = 98304
N_REP = 16
N_FSDP = 32


def spiked(array, own_key, source, target, shards_of, factor):
    def block_of(dim):
        return (jnp.arange(array.shape[dim]) // (array.shape[dim] // shards_of)).reshape((-1,) + (1,) * (array.ndim - 1 - dim))

    near = jax.random.permutation(own_key, shards_of)[block_of(target)]
    far = (block_of(target) + shards_of // 2) % shards_of
    return jnp.where((block_of(source) == near) | (block_of(source) == far), factor * array, array)


def level_of(own_key, shape, shards, low, top_value):
    loudness, own = 1.0, jax.random.fold_in(own_key, 6)
    for position, shards_of in shards:
        steps = jnp.exp(jax.random.uniform(jax.random.fold_in(own, position), (shards_of,), jnp.float32, low / len(shards), top_value / len(shards)))
        loudness = loudness * jnp.repeat(steps, shape[position] // shards_of).reshape([-1 if axis == position else 1 for axis in range(len(shape))])
    return loudness


def normal_values(key, extent, spread, reach, split=(), kind=jnp.bfloat16):
    entries = jax.random.normal(key, extent, jnp.float32) * spread
    if len(split) > 0:
        entries = level_of(key, extent, split, -0.22, 0.18) * entries
    return jnp.clip(entries, min=-reach, max=reach).astype(kind)


def bell_draw_with(own_key, extent, scale, most, pieces, heavy, kind=jnp.bfloat16):
    result = scale * jax.random.normal(own_key, extent, jnp.float32)
    if pieces:
        result = result * level_of(own_key, extent, pieces, -0.22, 0.18)
    return jnp.clip(spiked(result, jax.random.fold_in(own_key, 3), *heavy), -most, most).astype(kind)


def setup_inputs(seed: int = 0) -> dict:
    key_of = jax.random.split(jax.random.key(seed), 6)
    hid_acts = bell_draw_with(key_of[0], (LAYERS, TOKENS, ROWS), 1.0, 16.0, ((1, 512),), (1, 2, 64, 4.0))
    out_cot = normal_values(key_of[1], (LAYERS, TOKENS, D), 1.0, 6.0, ((1, 512),))
    momentum = normal_values(key_of[2], (N_REP, ROWS, LAYERS, D), 1.0, 6.0, ((0, 16), (1, 32)), jnp.float32)
    weight = normal_values(key_of[3], (ROWS, LAYERS, D), ROWS ** -0.5, 0.25, ((0, 32),))
    next_acts = normal_values(key_of[4], (LAYERS, TOKENS, ROWS), 1.0, 6.0, ((1, 512),))
    return {"hid_acts": hid_acts, "out_cot": out_cot, "momentum": momentum, "weight": weight, "next_acts": next_acts}


def cosine_table(length, kept_count):
    frequency = jnp.arange(kept_count, dtype=jnp.float32)[:, None]
    sample = jnp.arange(length, dtype=jnp.float32)[None, :]
    cosines = jnp.cos(jnp.pi * (2.0 * sample + 1.0) * frequency / (2.0 * length)) * jnp.sqrt(2.0 / length)
    return jnp.where(frequency == 0.0, cosines * jnp.sqrt(0.5), cosines)

def encode(values, cosine_rows):
    shaped = values.reshape(values.shape[:-1] + (values.shape[-1] // cosine_rows.shape[1], cosine_rows.shape[1]))
    return jnp.einsum('...c,kc->...k', shaped, cosine_rows, precision=lax.Precision.HIGHEST)

def decode(coeffs, cosine_rows):
    shaped = jnp.einsum('...k,kc->...c', coeffs, cosine_rows, precision=lax.Precision.HIGHEST)
    return shaped.reshape(shaped.shape[:-2] + (shaped.shape[-2] * shaped.shape[-1],))

def reference(hid_acts, out_cot, momentum, weight, next_acts):
    group_tokens = TOK_DEV * N_FSDP
    norm_factor = 1.0 / math.sqrt(group_tokens)
    grads = []
    for group in range(N_REP):
        acts_part = hid_acts[:, group * group_tokens:(group + 1) * group_tokens, :].astype(jnp.float32)
        cot_part = out_cot[:, group * group_tokens:(group + 1) * group_tokens, :].astype(jnp.float32)
        acts_runs = acts_part.reshape(LAYERS, N_FSDP, TOK_DEV, ROWS)
        cot_runs = cot_part.reshape(LAYERS, N_FSDP, TOK_DEV, D)
        partial_value = (jnp.einsum('lstr,lstd->srld', acts_runs, cot_runs) * norm_factor).astype(jnp.bfloat16)
        partial_value = lax.optimization_barrier(partial_value)
        grads.append(lax.optimization_barrier(jnp.sum(partial_value.astype(jnp.float32), axis=0)))
    grad = jnp.stack(grads, axis=0)
    blended = 0.9 * momentum + grad
    cosine_rows = cosine_table(SPAN, KEEP)
    coeffs = encode(blended, cosine_rows)
    new_momentum = blended - decode(coeffs, cosine_rows)
    mean_coeffs = lax.optimization_barrier(jnp.sum(coeffs, axis=0)) / N_REP
    new_weight = (weight.astype(jnp.float32) - 0.5 * decode(mean_coeffs, cosine_rows)).astype(jnp.bfloat16)
    weight_wide = new_weight.astype(jnp.float32)
    outputs = []
    for group in range(N_REP):
        group_acts = next_acts[:, group * group_tokens:(group + 1) * group_tokens, :].astype(jnp.float32)
        outputs.append(jnp.einsum('ltr,rld->ltd', group_acts, weight_wide).astype(jnp.bfloat16))
    next_out = jnp.concatenate(outputs, axis=1)
    return (next_out, new_momentum)
```

```python
import math

import jax
import jax.numpy as jnp
import numpy as np
from jax import lax
from jax.experimental import pallas as pl
from jax.experimental.pallas import tpu as pltpu
from jax.sharding import PartitionSpec as P

SPAN = 256
KEEP = 32
HIGH = SPAN - KEEP
TOK = 192
ROWS = 448
D = 4608
BLOCKS = D // SPAN
OWN = 14
HALF = 224
NY, NZ, NX = 8, 8, 4
SLICE = D // 4
LOW_AT = 4096
CT = LOW_AT + 640
NORM = 1.0 / math.sqrt(TOK * 32)
F32, BF16 = jnp.float32, jnp.bfloat16
HI = lax.Precision.HIGHEST


def tables():
    k = np.arange(SPAN, dtype=np.float64)[:, None]
    n = np.arange(SPAN, dtype=np.float64)[None, :]
    dct = np.cos(np.pi * (2.0 * n + 1.0) * k / (2.0 * SPAN)) * np.sqrt(2.0 / SPAN)
    dct[0] *= np.sqrt(0.5)
    low, high = dct[:KEEP], dct[KEEP:]
    forward = np.concatenate([high, low], axis=0).T
    back = np.concatenate([high, np.zeros((KEEP, SPAN))], axis=0)
    low_t = np.tile(low.T, (1, 4))
    diag = np.zeros((128, 1024))
    for i in range(4):
        diag[32 * i : 32 * i + 32, 256 * i : 256 * i + 256] = low
    diag = np.concatenate([diag, diag], axis=0)
    return (
        jnp.asarray(forward, BF16),
        jnp.asarray(back, BF16),
        jnp.asarray(low_t, F32),
        jnp.asarray(low, F32),
        jnp.asarray(diag, BF16),
    )


def dot(a, b, contract=((1,), (0,)), precision=None):
    return lax.dot_general(
        a, b, (contract, ((), ())), precision=precision, preferred_element_type=F32
    )


def iota(shape, dim):
    return lax.broadcasted_iota(jnp.int32, shape, dim)


def cdiv14(w):
    return (w >= 14).astype(jnp.int32)


FOUND = ((0,), (-1, 1), (-2, 2), (-3, 3), (-4,))
UP = (0, -1, -2, -3)


def slot_of(o):
    return o + 4


def kernel(
    hid_h, cot_h, mom_h, w_h, act_h, fwd_h, back_h, lowt_h, low_h, diag_h,
    out_ref, nm_ref,
    cot, hid, acts, mom, wraw, fwd, back, lowt, low, diag,
    ct, lowf, lhs, gram, parts, ring, xs, xr, keep, m2, nm2, high8,
    wsh, wx, wbuf, cbuf, cxr, cx, czr, cz, cyr, mbuf, call, actw, actc, acc,
    lsem, hid_s, ct_s, ring_s, x2_s, w0_s, wy_s, wza_s, wzb_s, wzf_s, wxx_s, wsib_s,
    c1_s, c2_s, c3_s, c4_s, c5_s, c6_s,
):
    rep, f = lax.axis_index("rep"), lax.axis_index("fsdp")
    xlo, z = rep // NZ, rep % NZ
    y, xhi, c = f // 4, (f // 2) % 2, f % 2
    x = xhi * 2 + xlo

    def dev(dx=0, dy=0, dz=0, dc=0):
        xx, yy, zz, cc = (x + dx + NX) % NX, (y + dy + NY) % NY, (z + dz + NZ) % NZ, (c + dc) % 2
        return ((xx % 2) * NZ + zz, (yy * 2 + xx // 2) * 2 + cc)

    pending = []

    def send(src, dst, sems, index, to):
        copy = pltpu.make_async_remote_copy(
            src_ref=src, dst_ref=dst, send_sem=sems.at[(0,) + index], recv_sem=sems.at[(1,) + index],
            device_id=to, device_id_type=pl.DeviceIdType.MESH,
        )
        copy.start()
        pending.append(copy)

    def wait(dst, sems, index):
        pltpu.make_async_remote_copy(
            src_ref=dst, dst_ref=dst, send_sem=sems.at[(0,) + index], recv_sem=sems.at[(1,) + index],
            device_id=dev(dc=1), device_id_type=pl.DeviceIdType.MESH,
        ).wait_recv()

    loads = {}
    for i, (name, src, dst) in enumerate((
        ("w", w_h, wraw), ("hid", hid_h.at[0], hid.at[pl.ds(0, TOK)]), ("fwd", fwd_h, fwd),
        ("cot", cot_h.at[0], cot), ("mom", mom_h, mom), ("lowt", lowt_h, lowt), ("low", low_h, low),
        ("acts", act_h.at[0], acts), ("back", back_h, back), ("diag", diag_h, diag),
    )):
        loads[name] = pltpu.make_async_copy(src, dst, lsem.at[i])
        loads[name].start()

    barrier = pltpu.get_barrier_semaphore()
    friends = [dev(dc=1)]
    friends += [dev(dy=i) for i in range(1, NY)]
    friends += [dev(dz=i) for i in range(1, NZ)]
    friends += [dev(dx=i) for i in range(1, NX)]
    for friend in friends:
        pl.semaphore_signal(barrier, inc=1, device_id=friend, device_id_type=pl.DeviceIdType.MESH)

    loads["w"].wait()
    wsh[...] = jnp.concatenate([wraw[...], jnp.zeros((2, D), BF16)], axis=0)
    m2[...] = jnp.zeros_like(m2)
    loads["mom"].wait()
    for b in range(BLOCKS):
        for h in range(2):
            m2[pl.ds(16 * b, OWN), pl.ds(128 * h, 128)] = mom[pl.ds(2 * b + h, OWN, stride=36), :]

    pl.semaphore_wait(barrier, len(friends))

    sig = z % 4
    kap = xlo

    def cols(s):
        return pl.ds(pl.multiple_of(((s + 4) % 4) * SLICE, 128), SLICE)

    def wslice(o, s, k=None):
        return wbuf.at[c, kap if k is None else k, (y + o + NY) % NY, :, cols(s)]

    def wfull(o, k, core=None):
        return wbuf.at[c if core is None else core, k, (y + o + NY) % NY]

    cross = lax.rem(x + 3 * (1 - xlo) + xlo, NX)
    cross_dev = ((cross % 2) * NZ + z, (y * 2 + cross // 2) * 2 + c)
    loads["hid"].wait()
    send(hid.at[pl.ds(0, TOK)], hid.at[pl.ds(TOK, TOK)], hid_s, (0,), dev(dc=1))
    send(wsh.at[:, cols(sig)], wx, w0_s, (0,), cross_dev)

    loads["fwd"].wait()
    loads["cot"].wait()
    lane = iota((TOK, 128), 1)
    table = fwd[...]
    seen = set()

    def transform(b):
        full = dot(cot[:, pl.ds(SPAN * b, SPAN)], table)
        first, second = full[:, :128], full[:, 128:]
        u, place = b // 4, 32 * (b % 4)
        turned = pltpu.roll(second, (place - 96) % 128, 1) if place != 96 else second
        mine = (lane >= place) & (lane < place + 32)
        at = pl.ds(128 * u, 128)
        lowf[:, at] = jnp.where(mine, turned, lowf[:, at] if u in seen else 0.0)
        seen.add(u)
        return first, second

    for h in range(2):
        first, second = transform(9 * h + 8)
        high8[h, :, pl.ds(0, 128)] = first
        high8[h, :, pl.ds(128, 128)] = second
    for s in range(4):
        for q in range(4):
            h, j = q // 2, 4 * (q % 2) + s
            first, second = transform(9 * h + j)
            if j < 7:
                extra = high8[h, :, pl.ds(128 * (j // 4), 128)]
                shift = (96 - 32 * (j % 4)) % 128
                extra = pltpu.roll(extra, shift, 1) if shift else extra
            else:
                extra = jnp.zeros_like(second)
            at = 1024 * s + 256 * q
            ct[pl.ds(0, TOK), pl.ds(at, 128)] = first.astype(BF16)
            ct[pl.ds(0, TOK), pl.ds(at + 128, 128)] = jnp.where(lane < 96, second, extra).astype(BF16)
        part = pl.ds(1024 * s, 1024)
        send(ct.at[pl.ds(0, TOK), part], ct.at[pl.ds(TOK, TOK), part], ct_s, (s,), dev(dc=1))
    ct[pl.ds(0, TOK), pl.ds(LOW_AT, 640)] = lowf[...].astype(BF16)
    part = pl.ds(LOW_AT, 640)
    send(ct.at[pl.ds(0, TOK), part], ct.at[pl.ds(TOK, TOK), part], ct_s, (4,), dev(dc=1))

    wait(wx, w0_s, (0,))
    own = wsh[:, cols(sig)]
    wslice(0, sig)[...] = jnp.where(jnp.broadcast_to(kap == xhi, own.shape), own, wx[...])

    def wy_send(k):
        send(wslice(1 - k, sig), wslice(1 - k, sig), wy_s, (0, k - 1), dev(dy=1))
        if k < 4:
            send(wslice(k - 1, sig), wslice(k - 1, sig), wy_s, (1, k - 1), dev(dy=-1))

    def wy_wait(k):
        wait(wslice(-k, sig), wy_s, (0, k - 1))
        if k < 4:
            wait(wslice(k, sig), wy_s, (1, k - 1))

    def wz_send(k):
        for o in FOUND[k]:
            send(wslice(o, sig), wslice(o, sig), wza_s, (slot_of(o),), dev(dz=1))
            send(wslice(o, sig), wslice(o, sig), wzb_s, (slot_of(o),), dev(dz=-1))

    def wz_pass(k):
        for o in FOUND[k]:
            wait(wslice(o, sig - 1), wza_s, (slot_of(o),))
            wait(wslice(o, sig + 1), wzb_s, (slot_of(o),))
            if o in UP:
                send(wslice(o, sig - 1), wslice(o, sig - 1), wzf_s, (slot_of(o),), dev(dz=1))
            else:
                send(wslice(o, sig + 1), wslice(o, sig + 1), wzf_s, (slot_of(o),), dev(dz=-1))

    def wx_send(k):
        for o in FOUND[k]:
            wait(wslice(o, sig + 2), wzf_s, (slot_of(o),))
            send(wfull(o, kap), wfull(o, kap), wxx_s, (slot_of(o),), dev(dx=1 if o in UP else -1))
            send(wfull(o, kap), wfull(o, kap), wsib_s, (0, slot_of(o)), dev(dc=1))

    def wx_wait(k):
        for o in FOUND[k]:
            wait(wfull(o, 1 - kap), wxx_s, (slot_of(o),))
            send(wfull(o, 1 - kap), wfull(o, 1 - kap), wsib_s, (1, slot_of(o)), dev(dc=1))

    def wsib_wait(k):
        for o in FOUND[k]:
            wait(wfull(o, kap, 1 - c), wsib_s, (0, slot_of(o)))
            wait(wfull(o, 1 - kap, 1 - c), wsib_s, (1, slot_of(o)))

    def w_step(i):
        if 1 <= i <= 4:
            wy_wait(i)
            if i < 4:
                wy_send(i + 1)
            wz_send(i)
        if 0 <= i - 1 <= 4:
            wz_pass(i - 1)
        if 0 <= i - 2 <= 4:
            wx_send(i - 2)
        if 0 <= i - 3 <= 4:
            wx_wait(i - 3)

    wy_send(1)
    wz_send(0)

    wait(hid.at[pl.ds(TOK, TOK)], hid_s, (0,))
    both = hid[...]
    for at, rows, width, lead in ((0, 256, 32, 0), (256, 256, 32, 4), (512, 224, 28, 0)):
        for g in range(NY):
            row, col = iota((width, ROWS), 0), iota((width, ROWS), 1)
            w = row - lead
            good = (w >= 0) & (w < 28)
            target = 56 * g + 14 * c + w + 14 * cdiv14(w)
            gram[pl.ds(0, width), pl.ds(0, ROWS)] = jnp.where(good & (col == target), 1.0, 0.0)
            lhs[pl.ds(at + width * g, width)] = dot(
                gram[pl.ds(0, width), pl.ds(0, ROWS)].astype(BF16), both, ((1,), (1,))
            )
    left = [lhs[pl.ds(256 * i, 256)].astype(BF16) for i in range(2)]

    def ring_send(s, k):
        d = 1 if s % 2 == 0 else -1
        src = parts.at[s, (y - d + NY) % NY] if k == 0 else ring.at[s, k - 1]
        send(src, ring.at[s, k], ring_s, (s, k), dev(dy=d))

    def ring_step(s, k):
        d = 1 if s % 2 == 0 else -1
        wait(ring.at[s, k], ring_s, (s, k))
        owner = (y - d * (2 + k) + 2 * NY) % NY
        total = ring[s, k].astype(F32) + parts[s, owner].astype(F32)
        ring[s, k] = total.astype(BF16)
        if k < 6:
            ring_send(s, k + 1)

    for s in range(4):
        wait(ct.at[pl.ds(TOK, TOK), pl.ds(1024 * s, 1024)], ct_s, (s,))
        for q in range(4):
            gram[pl.ds(256 * q, 256), pl.ds(0, 256)] = (
                dot(left[q % 2], ct[:, pl.ds(1024 * s + 256 * q, 256)]) * NORM
            )
        for g in range(NY):
            pieces = []
            for pair in range(2):
                a = gram[pl.ds(512 * pair + 32 * g, 32), pl.ds(0, 256)]
                b = gram[pl.ds(512 * pair + 256 + 32 * g, 32), pl.ds(0, 256)]
                pieces += [a[:24], a[24:] + b[:8], b[8:]]
            parts[s, g] = jnp.concatenate(pieces, axis=0).astype(BF16)
        ring_send(s, 0)

    loads["lowt"].wait()
    loads["low"].wait()
    mine = m2[...]
    kept = dot(mine, lowt[...], precision=HI)
    nm2[...] = 0.9 * (mine - dot(kept[:, :KEEP], low[...], precision=HI))
    lane16 = iota((16, 128), 1)
    tiles = []
    for u in range(5):
        tile = jnp.zeros((16, 128), F32)
        for i in range(4):
            b = 4 * u + i
            if b < BLOCKS:
                good = (lane16 >= 32 * i) & (lane16 < 32 * i + 32)
                tile = jnp.where(good, 0.9 * kept[16 * b : 16 * b + 16], tile)
        tiles.append(tile)
    spread = jnp.concatenate(tiles, axis=1)
    row, col = iota((HALF, 16), 0), iota((HALF, 16), 1)
    place = jnp.where((row == OWN * (2 * y + xhi) + col) & (col < OWN), 1.0, 0.0)
    wait(ct.at[pl.ds(TOK, TOK), pl.ds(LOW_AT, 640)], ct_s, (4,))
    local = dot(lhs[pl.ds(512, HALF)].astype(BF16), ct[:, pl.ds(LOW_AT, 640)]) * NORM
    local = local + dot(place, spread, precision=HI)
    for rt in range(14):
        for u in range(4):
            cbuf[4 * rt + u] = local[16 * rt : 16 * rt + 16, 128 * u : 128 * u + 128].astype(BF16)
    for i in range(7):
        a = local[32 * i : 32 * i + 16, 512:640]
        b = local[32 * i + 16 : 32 * i + 32, 512:640]
        cbuf[56 + i] = jnp.where(lane16 < 64, a, pltpu.roll(b, 64, 1)).astype(BF16)
    cbuf[63] = jnp.zeros((16, 128), BF16)

    def c1_send():
        for i in range(1, NX):
            to = (x + i) % NX
            send(cbuf.at[pl.ds(16 * to, 16)], cxr.at[i - 1], c1_s, (i - 1,), dev(dx=i))

    def c2_send():
        total = cbuf[pl.ds(16 * x, 16)].astype(F32)
        for i in range(1, NX):
            wait(cxr.at[i - 1], c1_s, (i - 1,))
            total = total + cxr[i - 1].astype(F32)
        cx[...] = total.astype(BF16)
        for i in range(1, NZ):
            send(cx.at[pl.ds(2 * ((z + i) % NZ), 2)], czr.at[i - 1], c2_s, (i - 1,), dev(dz=i))

    def c3_send():
        total = cx[pl.ds(2 * z, 2)].astype(F32)
        for i in range(1, NZ):
            wait(czr.at[i - 1], c2_s, (i - 1,))
            total = total + czr[i - 1].astype(F32)
        cz[...] = total.astype(BF16)
        for i in range(1, NY):
            send(cz, cyr.at[i - 1], c3_s, (i - 1,), dev(dy=i))

    def piece(zz):
        return mbuf.at[c, pl.ds(16 * x + 2 * ((zz + NZ) % NZ), 2)]

    def c4_send():
        total = cz[...].astype(F32)
        for i in range(1, NY):
            wait(cyr.at[i - 1], c3_s, (i - 1,))
            total = total + cyr[i - 1].astype(F32)
        piece(z)[...] = (total * (1.0 / 16.0)).astype(BF16)
        for i in range(1, NZ):
            send(piece(z), piece(z), c4_s, (i - 1,), dev(dz=i))

    def strip(xx, core):
        return mbuf.at[core, pl.ds(16 * ((xx + NX) % NX), 16)]

    def c5_send():
        for i in range(1, NZ):
            wait(piece(z - i), c4_s, (i - 1,))
        for i in range(1, NX):
            send(strip(x, c), strip(x, c), c5_s, (i - 1,), dev(dx=i))
        send(strip(x, c), strip(x, c), c6_s, (0,), dev(dc=1))

    def c6_send():
        for i in range(1, NX):
            wait(strip(x - i, c), c5_s, (i - 1,))
            send(strip(x - i, c), strip(x - i, c), c6_s, (i,), dev(dc=1))

    def c_done():
        for i in range(NX):
            wait(strip(x - i, 1 - c), c6_s, (i,))

    c1_send()

    loads["acts"].wait()
    a = acts[...]
    row, col = iota((ROWS, HALF), 0), iota((ROWS, HALF), 1)
    for core in range(2):
        pick = jnp.zeros((ROWS, HALF), F32)
        for g in range(NY):
            w = col - 28 * g
            good = (w >= 0) & (w < 28)
            target = 56 * g + 14 * core + w + 14 * cdiv14(w)
            pick = jnp.where(good & (row == target), 1.0, pick)
        actc[core] = dot(a, pick.astype(BF16)).astype(BF16)
        row2, col2 = iota((ROWS, 256), 0), iota((ROWS, 256), 1)
        j, t = col2 % 16, col2 // 16
        target = 56 * (t % 8) + 28 * (t // 8) + 14 * core + j
        pick = jnp.where((j < OWN) & (row2 == target), 1.0, 0.0)
        actw[:, pl.ds(256 * core, 256)] = dot(a, pick.astype(BF16)).astype(BF16)

    def ring_all(k):
        for s in range(4):
            ring_step(s, k)

    ring_all(0)
    w_step(1)
    ring_all(1)
    c2_send()
    w_step(2)
    ring_all(2)
    c3_send()
    w_step(3)
    ring_all(3)
    c4_send()
    w_step(4)
    ring_all(4)
    c5_send()
    w_step(5)
    ring_all(5)
    w_step(6)
    c6_send()

    row, col = iota((64, 112), 0), iota((64, 112), 1)
    j, q16 = row % 16, row // 16

    def pick_rows(hi):
        return jnp.where((j < OWN) & (col == 28 * q16 + 14 * hi + j), 1.0, 0.0).astype(BF16)

    for s in range(4):
        ring_step(s, 6)
        chunk = ring[s, 6]
        xs[s] = dot(pick_rows(1 - xhi), chunk).astype(BF16)
        send(xs.at[s], xr.at[s], x2_s, (s,), dev(dx=2))
        keep[s] = dot(pick_rows(xhi), chunk)

    w_step(7)
    for k in range(5):
        wsib_wait(k)
    for core in range(2):
        for t in range(4):
            at = pl.ds(SLICE * t, SLICE)
            term = dot(actw[:, pl.ds(256 * core, 256)], wbuf[core, :, :, :, at].reshape(256, SLICE))
            acc[:, at] = term if core == 0 else acc[:, at] + term

    c_done()
    loads["diag"].wait()
    for core in range(2):
        for rt in range(14):
            for u in range(4):
                call[pl.ds(HALF * core + 16 * rt, 16), pl.ds(128 * u, 128)] = mbuf[core, 4 * rt + u]
        for i in range(7):
            tile = mbuf[core, 56 + i].astype(F32)
            at = HALF * core + 32 * i
            call[pl.ds(at, 16), pl.ds(512, 128)] = jnp.where(lane16 < 64, tile, 0.0).astype(BF16)
            call[pl.ds(at + 16, 16), pl.ds(512, 128)] = jnp.where(
                lane16 < 64, pltpu.roll(tile, 64, 1), 0.0
            ).astype(BF16)
    inner = dot(actc[0], call[pl.ds(0, HALF)]) + dot(actc[1], call[pl.ds(HALF, HALF)])
    inner = inner * 0.5
    top = inner.astype(BF16)
    rest = (inner - top.astype(F32)).astype(BF16)
    for u in range(5):
        width = 1024 if u < 4 else 512
        at = pl.ds(1024 * u, width)
        pair = jnp.concatenate([top[:, 128 * u : 128 * u + 128], rest[:, 128 * u : 128 * u + 128]], axis=1)
        out_ref[:, at] = (acc[:, at] - dot(pair, diag[:, pl.ds(0, width)])).astype(BF16)

    loads["back"].wait()
    inverse = back[...]
    eights = [[jnp.zeros((16, 128), F32) for _ in range(2)] for _ in range(2)]

    def to_space(values):
        big = values.astype(BF16)
        return dot(big, inverse) + dot((values - big.astype(F32)).astype(BF16), inverse)

    for s in range(4):
        wait(xr.at[s], x2_s, (s,))
        total = keep[s] + xr[s].astype(F32)
        space = to_space(total)
        for q in range(4):
            h, j = q // 2, 4 * (q % 2) + s
            at = pl.ds(16 * (9 * h + j), 16)
            nm2[at] = nm2[at] + space[16 * q : 16 * q + 16]
            if j < 7:
                tail = total[16 * q : 16 * q + 16, 128:]
                place = 32 * (j % 4)
                tail = pltpu.roll(tail, (place - 96) % 128, 1) if place != 96 else tail
                good = (lane16 >= place) & (lane16 < place + 32)
                eights[h][j // 4] = jnp.where(good, tail, eights[h][j // 4])
    for h in range(2):
        at = pl.ds(16 * (9 * h + 8), 16)
        nm2[at] = nm2[at] + to_space(jnp.concatenate(eights[h], axis=1))
    for b in range(BLOCKS):
        for h in range(2):
            nm_ref[pl.ds(2 * b + h, OWN, stride=36), :] = nm2[pl.ds(16 * b, OWN), pl.ds(128 * h, 128)]

    for copy in pending:
        copy.wait_send()


def local(hid_acts, out_cot, momentum, weight, next_acts):
    any_space = pl.BlockSpec(memory_space=pl.ANY)
    vmem = pl.BlockSpec(memory_space=pltpu.VMEM)
    dma = pltpu.SemaphoreType.DMA
    scratch = [
        pltpu.VMEM((TOK, D), BF16),
        pltpu.VMEM((2 * TOK, ROWS), BF16),
        pltpu.VMEM((TOK, ROWS), BF16),
        pltpu.VMEM((504, 128), F32),
        pltpu.VMEM((OWN, D), BF16),
        pltpu.VMEM((SPAN, SPAN), BF16),
        pltpu.VMEM((SPAN, SPAN), BF16),
        pltpu.VMEM((SPAN, 128), F32),
        pltpu.VMEM((KEEP, SPAN), F32),
        pltpu.VMEM((SPAN, 1024), BF16),
        pltpu.VMEM((2 * TOK, CT), BF16),
        pltpu.VMEM((TOK, 640), F32),
        pltpu.VMEM((736, 2 * TOK), F32),
        pltpu.VMEM((1024, 512), F32),
        pltpu.VMEM((4, NY, 112, 256), BF16),
        pltpu.VMEM((4, 7, 112, 256), BF16),
        pltpu.VMEM((4, 64, 256), BF16),
        pltpu.VMEM((4, 64, 256), BF16),
        pltpu.VMEM((4, 64, 256), F32),
        pltpu.VMEM((16 * BLOCKS, SPAN), F32),
        pltpu.VMEM((16 * BLOCKS, SPAN), F32),
        pltpu.VMEM((2, TOK, SPAN), F32),
        pltpu.VMEM((16, D), BF16),
        pltpu.VMEM((16, SLICE), BF16),
        pltpu.VMEM((2, 2, NY, 16, D), BF16),
        pltpu.VMEM((64, 16, 128), BF16),
        pltpu.VMEM((3, 16, 16, 128), BF16),
        pltpu.VMEM((16, 16, 128), BF16),
        pltpu.VMEM((7, 2, 16, 128), BF16),
        pltpu.VMEM((2, 16, 128), BF16),
        pltpu.VMEM((7, 2, 16, 128), BF16),
        pltpu.VMEM((2, 64, 16, 128), BF16),
        pltpu.VMEM((ROWS, 640), BF16),
        pltpu.VMEM((TOK, 512), BF16),
        pltpu.VMEM((2, TOK, HALF), BF16),
        pltpu.VMEM((TOK, D), F32),
        dma((10,)),
        dma((2, 1)),
        dma((2, 5)),
        dma((2, 4, 7)),
        dma((2, 4)),
        dma((2, 1)),
        dma((2, 2, 4)),
        dma((2, 8)),
        dma((2, 8)),
        dma((2, 8)),
        dma((2, 8)),
        dma((2, 2, 8)),
        dma((2, 3)),
        dma((2, 7)),
        dma((2, 7)),
        dma((2, 7)),
        dma((2, 3)),
        dma((2, 4)),
    ]
    out, nm = pl.pallas_call(
        kernel,
        out_shape=(
            jax.ShapeDtypeStruct((TOK, D), BF16),
            jax.ShapeDtypeStruct((504, 128), F32),
        ),
        in_specs=[any_space] * 10,
        out_specs=(vmem, vmem),
        scratch_shapes=scratch,
        compiler_params=pltpu.CompilerParams(
            collective_id=0, has_side_effects=True, vmem_limit_bytes=56 * 2**20
        ),
        name="step",
    )(
        hid_acts,
        out_cot,
        momentum.reshape(504, 128),
        weight.reshape(OWN, D),
        next_acts,
        *tables(),
    )
    return out[None], nm.reshape(1, OWN, 1, D)


def solution(mesh):
    return jax.shard_map(
        local,
        mesh=mesh,
        in_specs=(
            P(None, ("rep", "fsdp"), None),
            P(None, ("rep", "fsdp"), None),
            P("rep", "fsdp", None, None),
            P("fsdp", None, None),
            P(None, ("rep", "fsdp"), None),
        ),
        out_specs=(P(None, ("rep", "fsdp"), None), P("rep", "fsdp", None, None)),
        check_vma=False,
    )
```

```python
import math

import jax
import jax.numpy as jnp
import numpy as np
from jax import lax
from jax.experimental import pallas as pl
from jax.experimental.pallas import tpu as pltpu
from jax.sharding import PartitionSpec as P

SPAN = 256
KEEP = 32
HIGH = SPAN - KEEP
TOK = 192
ROWS = 448
D = 4608
BLOCKS = D // SPAN
OWN = 14
HALF = 224
NY, NZ, NX = 8, 8, 4
SLICE = D // 4
LOW_AT = 4096
CT = LOW_AT + 640
NORM = 1.0 / math.sqrt(TOK * 32)
F32, BF16 = jnp.float32, jnp.bfloat16
HI = lax.Precision.HIGHEST


def tables():
    k = np.arange(SPAN, dtype=np.float64)[:, None]
    n = np.arange(SPAN, dtype=np.float64)[None, :]
    dct = np.cos(np.pi * (2.0 * n + 1.0) * k / (2.0 * SPAN)) * np.sqrt(2.0 / SPAN)
    dct[0] *= np.sqrt(0.5)
    low, high = dct[:KEEP], dct[KEEP:]
    forward = np.concatenate([high, low], axis=0).T
    back = np.concatenate([high, np.zeros((KEEP, SPAN))], axis=0)
    low_t = np.tile(low.T, (1, 4))
    diag = np.zeros((128, 1024))
    for i in range(4):
        diag[32 * i : 32 * i + 32, 256 * i : 256 * i + 256] = low
    diag = np.concatenate([diag, diag], axis=0)
    return (
        jnp.asarray(forward, BF16),
        jnp.asarray(back, BF16),
        jnp.asarray(low_t, F32),
        jnp.asarray(low_t, BF16),
        jnp.asarray(low, F32),
        jnp.asarray(diag, BF16),
    )


def dot(a, b, contract=((1,), (0,)), precision=None):
    return lax.dot_general(
        a, b, (contract, ((), ())), precision=precision, preferred_element_type=F32
    )


def iota(shape, dim):
    return lax.broadcasted_iota(jnp.int32, shape, dim)


def over14(i):
    return (i * 4682) >> 16


FOUND = ((0,), (-1, 1), (-2, 2), (-3, 3), (-4,))
UP = (0, -1, -2, -3)
NEAR = 2


def slot_of(o):
    return o + 4


def hops(d, s):
    return 4 if (s < 2) == (d == 0) else 3


def kernel(
    hid_h, cot_h, mom_h, w_h, act_h, fwd_h, back_h, lowt_h, lowtb_h, low_h, diag_h,
    acc, pair_ref, nm2, diag,
    cot, hid, acts, mom, wraw, fwd, back, lowt, lowtb, low,
    ct, sel, lhs, gram, parts, ring, xs, xr, keep, m2, high8,
    wsh, wx, wbuf, cbuf, cxr, cx, czr, cz, cyr, mbuf, call, actw, actc,
    lsem, hid_s, ct_s, ring_s, x2_s, w0_s, wy_s, wza_s, wzb_s, wzf_s, wxx_s, wsib_s,
    c1_s, c2_s, c3_s, c4_s, c5_s, c6_s,
):
    rep, f = lax.axis_index("rep"), lax.axis_index("fsdp")
    xlo, z = rep // NZ, rep % NZ
    y, xhi, c = f // 4, (f // 2) % 2, f % 2
    x = xhi * 2 + xlo

    def dev(dx=0, dy=0, dz=0, dc=0):
        xx, yy, zz, cc = (x + dx + NX) % NX, (y + dy + NY) % NY, (z + dz + NZ) % NZ, (c + dc) % 2
        return ((xx % 2) * NZ + zz, (yy * 2 + xx // 2) * 2 + cc)

    pending = []

    def send(src, dst, sems, index, to):
        copy = pltpu.make_async_remote_copy(
            src_ref=src, dst_ref=dst, send_sem=sems.at[(0,) + index], recv_sem=sems.at[(1,) + index],
            device_id=to, device_id_type=pl.DeviceIdType.MESH,
        )
        copy.start()
        pending.append(copy)

    def wait(dst, sems, index):
        pltpu.make_async_remote_copy(
            src_ref=dst, dst_ref=dst, send_sem=sems.at[(0,) + index], recv_sem=sems.at[(1,) + index],
            device_id=dev(dc=1), device_id_type=pl.DeviceIdType.MESH,
        ).wait_recv()

    loads = {}
    for i, (name, src, dst) in enumerate((
        ("w", w_h, wraw), ("hid", hid_h.at[0], hid.at[pl.ds(0, TOK)]), ("lowtb", lowtb_h, lowtb),
        ("cot", cot_h.at[0], cot), ("fwd", fwd_h, fwd), ("mom", mom_h, mom), ("lowt", lowt_h, lowt),
        ("low", low_h, low), ("acts", act_h.at[0], acts), ("back", back_h, back), ("diag", diag_h, diag),
    )):
        loads[name] = pltpu.make_async_copy(src, dst, lsem.at[i])
        loads[name].start()

    barrier = pltpu.get_barrier_semaphore()
    friends = [dev(dc=1)]
    friends += [dev(dx=i) for i in range(1, NX)]
    friends += [dev(dy=i) for i in range(1, NY)]
    friends += [dev(dz=i) for i in range(1, NZ)]
    for friend in friends:
        pl.semaphore_signal(barrier, inc=1, device_id=friend, device_id_type=pl.DeviceIdType.MESH)

    i = iota((736, 1), 0)
    w = jnp.where(i < 256, i % 32, i % 32 - 4)
    k = jnp.where(i < 512, 28 * ((i % 256) // 32) + w, i - 512)
    good = (i >= 512) | ((w >= 0) & (w < 28))
    target = jnp.where(good, k + 14 * over14(jnp.maximum(k, 0)) + 14 * c, -1)
    sel[...] = jnp.where(iota((736, ROWS), 1) == target, 1.0, 0.0).astype(BF16)

    loads["w"].wait()
    wsh[...] = jnp.concatenate([wraw[...], jnp.zeros((2, D), BF16)], axis=0)
    loads["hid"].wait()
    pl.semaphore_wait(barrier, len(friends))

    sig = z % 4
    kap = xlo

    def cols(s):
        return pl.ds(pl.multiple_of(((s + 4) % 4) * SLICE, 128), SLICE)

    def wslice(o, s):
        return wbuf.at[c, kap, (y + o + NY) % NY, :, cols(s)]

    def wfull(o, k, core=None):
        return wbuf.at[c if core is None else core, k, (y + o + NY) % NY]

    cross = lax.rem(x + 3 * (1 - xlo) + xlo, NX)
    cross_dev = ((cross % 2) * NZ + z, (y * 2 + cross // 2) * 2 + c)
    send(wsh.at[:, cols(sig)], wx, w0_s, (0,), cross_dev)
    send(hid.at[pl.ds(0, TOK)], hid.at[pl.ds(TOK, TOK)], hid_s, (0,), dev(dc=1))

    loads["lowtb"].wait()
    loads["cot"].wait()
    lane = iota((TOK, 128), 1)
    low_table = lowtb[...]
    for u in range(5):
        tile = jnp.zeros((TOK, 128), F32)
        for i in range(4):
            b = 4 * u + i
            if b < BLOCKS:
                value = dot(cot[:, pl.ds(SPAN * b, SPAN)], low_table)
                tile = jnp.where((lane >= 32 * i) & (lane < 32 * i + 32), value, tile)
        ct[pl.ds(0, TOK), pl.ds(LOW_AT + 128 * u, 128)] = tile.astype(BF16)
    part = pl.ds(LOW_AT, 640)
    send(ct.at[pl.ds(0, TOK), part], ct.at[pl.ds(TOK, TOK), part], ct_s, (4,), dev(dc=1))

    loads["fwd"].wait()
    table = fwd[...]
    for h in range(2):
        high8[h] = dot(cot[:, pl.ds(SPAN * (9 * h + 8), SPAN)], table)
    for s in range(4):
        for q in range(4):
            h, j = q // 2, 4 * (q % 2) + s
            full = dot(cot[:, pl.ds(SPAN * (9 * h + j), SPAN)], table)
            if j < 7:
                extra = high8[h, :, pl.ds(128 * (j // 4), 128)]
                shift = (96 - 32 * (j % 4)) % 128
                extra = pltpu.roll(extra, shift, 1) if shift else extra
            else:
                extra = jnp.zeros((TOK, 128), F32)
            at = 1024 * s + 256 * q
            ct[pl.ds(0, TOK), pl.ds(at, 128)] = full[:, :128].astype(BF16)
            ct[pl.ds(0, TOK), pl.ds(at + 128, 128)] = jnp.where(lane < 96, full[:, 128:], extra).astype(BF16)
        part = pl.ds(1024 * s, 1024)
        send(ct.at[pl.ds(0, TOK), part], ct.at[pl.ds(TOK, TOK), part], ct_s, (s,), dev(dc=1))

    wait(wx, w0_s, (0,))
    own = wsh[:, cols(sig)]
    wslice(0, sig)[...] = jnp.where(jnp.broadcast_to(kap == xhi, own.shape), own, wx[...])

    def wz_send(k):
        for o in FOUND[k]:
            if o:
                wait(wslice(o, sig), wy_s, (slot_of(o),))
            send(wslice(o, sig), wslice(o, sig), wza_s, (slot_of(o),), dev(dz=1))
            send(wslice(o, sig), wslice(o, sig), wzb_s, (slot_of(o),), dev(dz=-1))
            if k < NEAR:
                send(wslice(o, sig), wslice(o, sig), wzf_s, (slot_of(o),), dev(dz=2 if o in UP else -2))

    def wz_pass(k):
        for o in FOUND[k]:
            wait(wslice(o, sig - 1), wza_s, (slot_of(o),))
            wait(wslice(o, sig + 1), wzb_s, (slot_of(o),))
            if k < NEAR:
                continue
            if o in UP:
                send(wslice(o, sig - 1), wslice(o, sig - 1), wzf_s, (slot_of(o),), dev(dz=1))
            else:
                send(wslice(o, sig + 1), wslice(o, sig + 1), wzf_s, (slot_of(o),), dev(dz=-1))

    def wx_send(k):
        for o in FOUND[k]:
            wait(wslice(o, sig + 2), wzf_s, (slot_of(o),))
            send(wfull(o, kap), wfull(o, kap), wxx_s, (slot_of(o),), dev(dx=1 if o in UP else -1))
            send(wfull(o, kap), wfull(o, kap), wsib_s, (0, slot_of(o)), dev(dc=1))

    def wx_wait(k):
        for o in FOUND[k]:
            wait(wfull(o, 1 - kap), wxx_s, (slot_of(o),))
            send(wfull(o, 1 - kap), wfull(o, 1 - kap), wsib_s, (1, slot_of(o)), dev(dc=1))

    def wsib_wait(k):
        for o in FOUND[k]:
            wait(wfull(o, kap, 1 - c), wsib_s, (0, slot_of(o)))
            wait(wfull(o, 1 - kap, 1 - c), wsib_s, (1, slot_of(o)))

    for i in (1, -1, 2, -2, 3, -3, 4):
        o = -i
        send(wslice(0, sig), wslice(0, sig), wy_s, (slot_of(o),), dev(dy=i))
    wz_send(0)

    wait(hid.at[pl.ds(TOK, TOK)], hid_s, (0,))
    lhs[...] = dot(sel[...], hid[...], ((1,), (1,))).astype(BF16)
    left = [lhs[pl.ds(256 * i, 256)] for i in range(2)]

    m2[...] = jnp.zeros_like(m2)
    loads["mom"].wait()
    for b in range(BLOCKS):
        for h in range(2):
            m2[pl.ds(16 * b, OWN), pl.ds(128 * h, 128)] = mom[pl.ds(2 * b + h, OWN, stride=36), :]
    loads["lowt"].wait()
    lane16 = iota((16, 128), 1)
    kept = dot(m2[...], lowt[...], precision=HI)
    tiles = []
    for u in range(5):
        tile = jnp.zeros((16, 128), F32)
        for i in range(4):
            b = 4 * u + i
            if b < BLOCKS:
                good = (lane16 >= 32 * i) & (lane16 < 32 * i + 32)
                tile = jnp.where(good, 0.9 * kept[16 * b : 16 * b + 16], tile)
        tiles.append(tile)
    spread = jnp.concatenate(tiles, axis=1)
    row, col = iota((HALF, 16), 0), iota((HALF, 16), 1)
    place = jnp.where((row == OWN * (2 * y + xhi) + col) & (col < OWN), 1.0, 0.0).astype(BF16)
    spread_top = spread.astype(BF16)
    placed = dot(place, spread_top) + dot(place, (spread - spread_top.astype(F32)).astype(BF16))
    wait(ct.at[pl.ds(TOK, TOK), pl.ds(LOW_AT, 640)], ct_s, (4,))
    local = dot(lhs[pl.ds(512, HALF)], ct[:, pl.ds(LOW_AT, 640)]) * NORM + placed
    for rt in range(14):
        for u in range(4):
            cbuf[4 * rt + u] = local[16 * rt : 16 * rt + 16, 128 * u : 128 * u + 128].astype(BF16)
    for i in range(7):
        a = local[32 * i : 32 * i + 16, 512:640]
        b = local[32 * i + 16 : 32 * i + 32, 512:640]
        cbuf[56 + i] = jnp.where(lane16 < 64, a, pltpu.roll(b, 64, 1)).astype(BF16)
    cbuf[63] = jnp.zeros((16, 128), BF16)

    def c1_send():
        for i in (1, 3, 2):
            to = (x + i) % NX
            send(cbuf.at[pl.ds(16 * to, 16)], cxr.at[i - 1], c1_s, (i - 1,), dev(dx=i))

    def c2_send():
        total = cbuf[pl.ds(16 * x, 16)].astype(F32)
        for i in (1, 3, 2):
            wait(cxr.at[i - 1], c1_s, (i - 1,))
            total = total + cxr[i - 1].astype(F32)
        cx[...] = total.astype(BF16)
        for i in range(1, NZ):
            send(cx.at[pl.ds(2 * ((z + i) % NZ), 2)], czr.at[i - 1], c2_s, (i - 1,), dev(dz=i))

    def c3_send():
        total = cx[pl.ds(2 * z, 2)].astype(F32)
        for i in range(1, NZ):
            wait(czr.at[i - 1], c2_s, (i - 1,))
            total = total + czr[i - 1].astype(F32)
        cz[...] = total.astype(BF16)
        for i in range(1, NY):
            send(cz, cyr.at[i - 1], c3_s, (i - 1,), dev(dy=i))

    def piece(zz):
        return mbuf.at[c, pl.ds(16 * x + 2 * ((zz + NZ) % NZ), 2)]

    def c4_send():
        total = cz[...].astype(F32)
        for i in range(1, NY):
            wait(cyr.at[i - 1], c3_s, (i - 1,))
            total = total + cyr[i - 1].astype(F32)
        piece(z)[...] = (total * (1.0 / 16.0)).astype(BF16)
        for i in range(1, NZ):
            send(piece(z), piece(z), c4_s, (i - 1,), dev(dz=i))

    def strip(xx, core):
        return mbuf.at[core, pl.ds(16 * ((xx + NX) % NX), 16)]

    def c5_send():
        for i in range(1, NZ):
            wait(piece(z - i), c4_s, (i - 1,))
        for i in (1, 3, 2):
            send(strip(x, c), strip(x, c), c5_s, (i - 1,), dev(dx=i))
        send(strip(x, c), strip(x, c), c6_s, (0,), dev(dc=1))

    def c6_send():
        for i in (1, 3, 2):
            wait(strip(x - i, c), c5_s, (i - 1,))
            send(strip(x - i, c), strip(x - i, c), c6_s, (i,), dev(dc=1))

    def c_done():
        for i in range(NX):
            wait(strip(x - i, 1 - c), c6_s, (i,))

    c1_send()

    def towards(d, steps):
        return (y + (steps if d == 0 else -steps) + NY) % NY

    def first_hop(s):
        wait(ct.at[pl.ds(TOK, TOK), pl.ds(1024 * s, 1024)], ct_s, (s,))
        for q in range(4):
            gram[pl.ds(256 * q, 256)] = dot(left[q % 2], ct[:, pl.ds(1024 * s + 256 * q, 256)]) * NORM
        for g in range(NY):
            pieces = []
            for pair in range(2):
                a = gram[pl.ds(512 * pair + 32 * g, 32)]
                b = gram[pl.ds(512 * pair + 256 + 32 * g, 32)]
                pieces += [a[:24], a[24:] + b[:8], b[8:]]
            parts[s, g] = jnp.concatenate(pieces, axis=0).astype(BF16)
        for d in range(2):
            send(parts.at[s, towards(d, hops(d, s))], ring.at[d, s, 0], ring_s, (d, s, 0), dev(dy=1 - 2 * d))

    def next_hop(d, s, k):
        wait(ring.at[d, s, k - 1], ring_s, (d, s, k - 1))
        left_over = hops(d, s) - k
        if left_over:
            total = ring[d, s, k - 1].astype(F32) + parts[s, towards(d, left_over)].astype(F32)
            ring[d, s, k - 1] = total.astype(BF16)
            send(ring.at[d, s, k - 1], ring.at[d, s, k], ring_s, (d, s, k), dev(dy=1 - 2 * d))

    row, col = iota((64, 112), 0), iota((64, 112), 1)
    j, q16 = row % 16, row // 16

    def pick_rows(hi):
        return jnp.where((j < OWN) & (col == 28 * q16 + 14 * hi + j), 1.0, 0.0).astype(BF16)

    theirs, ours = pick_rows(1 - xhi), pick_rows(xhi)

    def exchange(s):
        total = parts[s, y].astype(F32)
        for d in range(2):
            total = total + ring[d, s, hops(d, s) - 1].astype(F32)
        chunk = total.astype(BF16)
        xs[s] = dot(theirs, chunk).astype(BF16)
        send(xs.at[s], xr.at[s], x2_s, (s,), dev(dx=2))
        keep[s] = dot(ours, chunk)

    def momentum_rest():
        loads["low"].wait()
        nm2[...] = 0.9 * (m2[...] - dot(kept[:, :KEEP], low[...], precision=HI))

    def left_two():
        loads["acts"].wait()
        a = acts[...]
        for core in range(2):
            i = iota((1, HALF), 1)
            target = i + 14 * over14(i) + 14 * core
            pick = jnp.where(iota((ROWS, HALF), 0) == target, 1.0, 0.0)
            actc[core] = dot(a, pick.astype(BF16)).astype(BF16)
            i = iota((1, 256), 1)
            j, t = i % 16, i // 16
            target = jnp.where(j < OWN, 56 * (t % 8) + 28 * (t // 8) + 14 * core + j, -1)
            pick = jnp.where(iota((ROWS, 256), 0) == target, 1.0, 0.0)
            actw[:, pl.ds(256 * core, 256)] = dot(a, pick.astype(BF16)).astype(BF16)

    for s in range(4):
        first_hop(s)

    events = [
        (8.0, momentum_rest, ()),
        (8.1, left_two, ()),
        (9, wz_pass, (0,)),
        (9.2, wz_send, (1,)),
        (10.7, wz_send, (2,)),
        (11.5, c2_send, ()),
        (11.6, wx_send, (0,)),
        (12.2, wz_send, (3,)),
        (12.3, wz_pass, (1,)),
        (13.5, wz_send, (4,)),
        (13.7, wz_pass, (2,)),
        (12.4, wx_send, (1,)),
        (16, c3_send, ()),
        (16.05, wz_pass, (3,)),
        (17, wz_pass, (4,)),
        (17.1, wx_send, (2,)),
        (16, wx_wait, (0,)),
        (19.5, wx_send, (3,)),
        (18.5, wx_wait, (1,)),
        (20.5, c4_send, ()),
        (21, wx_send, (4,)),
        (23, wx_wait, (2,)),
        (25, c5_send, ()),
        (26, wx_wait, (3,)),
        (27.5, wx_wait, (4,)),
        (29.5, c6_send, ()),
    ]
    at = 12
    for k in range(1, 5):
        for s in range(4):
            for d in range(2):
                if k <= hops(d, s):
                    events.append((at, next_hop, (d, s, k)))
            at += 1.4
    for s in range(4):
        events.append((at + 0.01 * s, exchange, (s,)))
    events.sort(key=lambda event: event[0])
    for _, run, given in events:
        run(*given)

    for k in range(5):
        wsib_wait(k)
    for t in range(4):
        at = pl.ds(SLICE * t, SLICE)
        acc[:, at] = dot(actw[...], wbuf[:, :, :, :, at].reshape(512, SLICE))
    loads["back"].wait()
    inverse = back[...]
    eights = [[jnp.zeros((16, 128), F32) for _ in range(2)] for _ in range(2)]

    def to_space(values):
        big = values.astype(BF16)
        return dot(big, inverse) + dot((values - big.astype(F32)).astype(BF16), inverse)

    for s in range(4):
        wait(xr.at[s], x2_s, (s,))
        total = keep[s] + xr[s].astype(F32)
        space = to_space(total)
        for q in range(4):
            h, j = q // 2, 4 * (q % 2) + s
            at = pl.ds(16 * (9 * h + j), 16)
            nm2[at] = nm2[at] + space[16 * q : 16 * q + 16]
            if j < 7:
                tail = total[16 * q : 16 * q + 16, 128:]
                spot = 32 * (j % 4)
                tail = pltpu.roll(tail, (spot - 96) % 128, 1) if spot != 96 else tail
                good = (lane16 >= spot) & (lane16 < spot + 32)
                eights[h][j // 4] = jnp.where(good, tail, eights[h][j // 4])
    for h in range(2):
        at = pl.ds(16 * (9 * h + 8), 16)
        nm2[at] = nm2[at] + to_space(jnp.concatenate(eights[h], axis=1))

    c_done()
    for core in range(2):
        for rt in range(14):
            for u in range(4):
                call[pl.ds(HALF * core + 16 * rt, 16), pl.ds(128 * u, 128)] = mbuf[core, 4 * rt + u]
        for i in range(7):
            tile = mbuf[core, 56 + i].astype(F32)
            at = HALF * core + 32 * i
            call[pl.ds(at, 16), pl.ds(512, 128)] = jnp.where(lane16 < 64, tile, 0.0).astype(BF16)
            call[pl.ds(at + 16, 16), pl.ds(512, 128)] = jnp.where(
                lane16 < 64, pltpu.roll(tile, 64, 1), 0.0
            ).astype(BF16)
    inner = dot(actc[0], call[pl.ds(0, HALF)]) + dot(actc[1], call[pl.ds(HALF, HALF)])
    inner = inner * 0.5
    top = inner.astype(BF16)
    rest = (inner - top.astype(F32)).astype(BF16)
    for u in range(5):
        pair_ref[:, pl.ds(256 * u, 128)] = top[:, 128 * u : 128 * u + 128]
        pair_ref[:, pl.ds(256 * u + 128, 128)] = rest[:, 128 * u : 128 * u + 128]

    loads["diag"].wait()
    for copy in pending:
        copy.wait_send()


def finish(acc, pair, nm2, diag, out_h, nm_h, out, nm, sems):
    copies = []
    for u in range(5):
        width = 1024 if u < 4 else 512
        at = pl.ds(1024 * u, width)
        out[:, at] = (acc[:, at] - dot(pair[:, pl.ds(256 * u, 256)], diag[:, pl.ds(0, width)])).astype(BF16)
        copies.append(pltpu.make_async_copy(out.at[:, at], out_h.at[:, at], sems.at[u]))
        copies[-1].start()
    for b in range(BLOCKS):
        for h in range(2):
            nm[pl.ds(2 * b + h, OWN, stride=36), :] = nm2[pl.ds(16 * b, OWN), pl.ds(128 * h, 128)]
    copies.append(pltpu.make_async_copy(nm, nm_h, sems.at[5]))
    copies[-1].start()
    for copy in copies:
        copy.wait()


def local(hid_acts, out_cot, momentum, weight, next_acts):
    any_space = pl.BlockSpec(memory_space=pl.ANY)
    hbm = pl.BlockSpec(memory_space=pltpu.HBM)
    vmem = pl.BlockSpec(memory_space=pltpu.VMEM)
    dma = pltpu.SemaphoreType.DMA
    scratch = [
        pltpu.VMEM((TOK, D), BF16),
        pltpu.VMEM((2 * TOK, ROWS), BF16),
        pltpu.VMEM((TOK, ROWS), BF16),
        pltpu.VMEM((504, 128), F32),
        pltpu.VMEM((OWN, D), BF16),
        pltpu.VMEM((SPAN, SPAN), BF16),
        pltpu.VMEM((SPAN, SPAN), BF16),
        pltpu.VMEM((SPAN, 128), F32),
        pltpu.VMEM((SPAN, 128), BF16),
        pltpu.VMEM((KEEP, SPAN), F32),
        pltpu.VMEM((2 * TOK, CT), BF16),
        pltpu.VMEM((736, ROWS), BF16),
        pltpu.VMEM((736, 2 * TOK), BF16),
        pltpu.VMEM((1024, 256), F32),
        pltpu.VMEM((4, NY, 112, 256), BF16),
        pltpu.VMEM((2, 4, 4, 112, 256), BF16),
        pltpu.VMEM((4, 64, 256), BF16),
        pltpu.VMEM((4, 64, 256), BF16),
        pltpu.VMEM((4, 64, 256), F32),
        pltpu.VMEM((16 * BLOCKS, SPAN), F32),
        pltpu.VMEM((2, TOK, SPAN), F32),
        pltpu.VMEM((16, D), BF16),
        pltpu.VMEM((16, SLICE), BF16),
        pltpu.VMEM((2, 2, NY, 16, D), BF16),
        pltpu.VMEM((64, 16, 128), BF16),
        pltpu.VMEM((3, 16, 16, 128), BF16),
        pltpu.VMEM((16, 16, 128), BF16),
        pltpu.VMEM((7, 2, 16, 128), BF16),
        pltpu.VMEM((2, 16, 128), BF16),
        pltpu.VMEM((7, 2, 16, 128), BF16),
        pltpu.VMEM((2, 64, 16, 128), BF16),
        pltpu.VMEM((ROWS, 640), BF16),
        pltpu.VMEM((TOK, 512), BF16),
        pltpu.VMEM((2, TOK, HALF), BF16),
        dma((11,)),
        dma((2, 1)),
        dma((2, 5)),
        dma((2, 2, 4, 4)),
        dma((2, 4)),
        dma((2, 1)),
        dma((2, 8)),
        dma((2, 8)),
        dma((2, 8)),
        dma((2, 8)),
        dma((2, 8)),
        dma((2, 2, 8)),
        dma((2, 3)),
        dma((2, 7)),
        dma((2, 7)),
        dma((2, 7)),
        dma((2, 3)),
        dma((2, 4)),
    ]
    given = (
        hid_acts,
        out_cot,
        momentum.reshape(504, 128),
        weight.reshape(OWN, D),
        next_acts,
        *tables(),
    )
    held = pl.pallas_call(
        kernel,
        out_shape=(
            pltpu.VMEM((TOK, D), F32),
            pltpu.VMEM((TOK, 5 * SPAN), BF16),
            pltpu.VMEM((16 * BLOCKS, SPAN), F32),
            pltpu.VMEM((SPAN, 1024), BF16),
        ),
        in_specs=[hbm] * 11,
        out_specs=(vmem,) * 4,
        scratch_shapes=scratch,
        compiler_params=pltpu.CompilerParams(
            collective_id=0, has_side_effects=True, vmem_limit_bytes=40 * 2**20
        ),
        name="step",
    )(
        *(pltpu.with_memory_space_constraint(a, pltpu.HBM) for a in given)
    )
    held = [pltpu.with_memory_space_constraint(a, pltpu.VMEM) for a in held]
    out, nm = pl.pallas_call(
        finish,
        out_shape=(
            jax.ShapeDtypeStruct((TOK, D), BF16),
            jax.ShapeDtypeStruct((504, 128), F32),
        ),
        in_specs=[vmem] * 4,
        out_specs=(any_space, any_space),
        scratch_shapes=[pltpu.VMEM((TOK, D), BF16), pltpu.VMEM((504, 128), F32), dma((6,))],
        compiler_params=pltpu.CompilerParams(vmem_limit_bytes=8 * 2**20),
        name="finish",
    )(*held)
    return out[None], nm.reshape(1, OWN, 1, D)


def solution(mesh):
    return jax.shard_map(
        local,
        mesh=mesh,
        in_specs=(
            P(None, ("rep", "fsdp"), None),
            P(None, ("rep", "fsdp"), None),
            P("rep", "fsdp", None, None),
            P("fsdp", None, None),
            P(None, ("rep", "fsdp"), None),
        ),
        out_specs=(P(None, ("rep", "fsdp"), None), P("rep", "fsdp", None, None)),
        check_vma=False,
    )
```

```python
import math

import jax
import jax.numpy as jnp
import numpy as np
from jax import lax
from jax.experimental import pallas as pl
from jax.experimental.pallas import tpu as pltpu
from jax.sharding import PartitionSpec as P

SPAN = 256
KEEP = 32
HIGH = SPAN - KEEP
TOK = 192
ROWS = 448
D = 4608
BLOCKS = D // SPAN
OWN = 14
HALF = 224
NY, NZ, NX = 8, 8, 4
SLICE = D // 4
LOW_AT = 4096
CT = LOW_AT + 640
NORM = 1.0 / math.sqrt(TOK * 32)
F32, BF16 = jnp.float32, jnp.bfloat16
HI = lax.Precision.HIGHEST


def tables():
    k = np.arange(SPAN, dtype=np.float64)[:, None]
    n = np.arange(SPAN, dtype=np.float64)[None, :]
    dct = np.cos(np.pi * (2.0 * n + 1.0) * k / (2.0 * SPAN)) * np.sqrt(2.0 / SPAN)
    dct[0] *= np.sqrt(0.5)
    low, high = dct[:KEEP], dct[KEEP:]
    forward = np.concatenate([high, low], axis=0).T
    back = np.concatenate([high, np.zeros((KEEP, SPAN))], axis=0)
    low_t = np.tile(low.T, (1, 4))
    diag = np.zeros((128, 1024))
    for i in range(4):
        diag[32 * i : 32 * i + 32, 256 * i : 256 * i + 256] = low
    diag = np.concatenate([diag, diag], axis=0)
    return (
        jnp.asarray(forward, BF16),
        jnp.asarray(back, BF16),
        jnp.asarray(low_t, F32),
        jnp.asarray(low_t, BF16),
        jnp.asarray(low, F32),
        jnp.asarray(diag, BF16),
    )


def dot(a, b, contract=((1,), (0,)), precision=None):
    return lax.dot_general(
        a, b, (contract, ((), ())), precision=precision, preferred_element_type=F32
    )


def iota(shape, dim):
    return lax.broadcasted_iota(jnp.int32, shape, dim)


def over14(i):
    return (i * 4682) >> 16


FOUND = ((0,), (-1, 1), (-2, 2), (-3, 3), (-4,))
UP = (0, -1, -2, -3)
NEAR = 2


def slot_of(o):
    return o + 4


def hops(d, s):
    return 4 if (s < 2) == (d == 0) else 3


def kernel(
    hid_h, cot_h, mom_h, w_h, act_h, fwd_h, back_h, lowt_h, lowtb_h, low_h, diag_h,
    acc, pair_ref, nm2, diag,
    cot, hid, acts, mom, wraw, fwd, back, lowt, lowtb, low,
    ct, sel, lhs, gram, parts, ring, xs, xr, keep, m2, high8,
    wsh, wx, wbuf, cbuf, cxr, cx, czr, cz, cyr, mbuf, call, actw, actc,
    lsem, hid_s, ct_s, ring_s, x2_s, w0_s, wy_s, wza_s, wzb_s, wzf_s, wxx_s, wsib_s,
    c1_s, c2_s, c3_s, c4_s, c5_s, c6_s,
):
    rep, f = lax.axis_index("rep"), lax.axis_index("fsdp")
    xlo, z = rep // NZ, rep % NZ
    y, xhi, c = f // 4, (f // 2) % 2, f % 2
    x = xhi * 2 + xlo

    def dev(dx=0, dy=0, dz=0, dc=0):
        xx, yy, zz, cc = (x + dx + NX) % NX, (y + dy + NY) % NY, (z + dz + NZ) % NZ, (c + dc) % 2
        return ((xx % 2) * NZ + zz, (yy * 2 + xx // 2) * 2 + cc)

    pending = []

    def send(src, dst, sems, index, to):
        copy = pltpu.make_async_remote_copy(
            src_ref=src, dst_ref=dst, send_sem=sems.at[(0,) + index], recv_sem=sems.at[(1,) + index],
            device_id=to, device_id_type=pl.DeviceIdType.MESH,
        )
        copy.start()
        pending.append(copy)

    def wait(dst, sems, index):
        pltpu.make_async_remote_copy(
            src_ref=dst, dst_ref=dst, send_sem=sems.at[(0,) + index], recv_sem=sems.at[(1,) + index],
            device_id=dev(dc=1), device_id_type=pl.DeviceIdType.MESH,
        ).wait_recv()

    loads = {}
    for i, (name, src, dst) in enumerate((
        ("w", w_h, wraw), ("hid", hid_h.at[0], hid.at[pl.ds(0, TOK)]), ("lowtb", lowtb_h, lowtb),
        ("cot", cot_h.at[0], cot), ("fwd", fwd_h, fwd), ("mom", mom_h, mom), ("lowt", lowt_h, lowt),
        ("low", low_h, low), ("acts", act_h.at[0], acts), ("back", back_h, back), ("diag", diag_h, diag),
    )):
        loads[name] = pltpu.make_async_copy(src, dst, lsem.at[i])
        loads[name].start()

    barrier = pltpu.get_barrier_semaphore()
    friends = [dev(dc=1)]
    friends += [dev(dx=i) for i in range(1, NX)]
    friends += [dev(dy=i) for i in range(1, NY)]
    friends += [dev(dz=i) for i in range(1, NZ)]
    for friend in friends:
        pl.semaphore_signal(barrier, inc=1, device_id=friend, device_id_type=pl.DeviceIdType.MESH)

    i = iota((736, 1), 0)
    w = jnp.where(i < 256, i % 32, i % 32 - 4)
    k = jnp.where(i < 512, 28 * ((i % 256) // 32) + w, i - 512)
    good = (i >= 512) | ((w >= 0) & (w < 28))
    target = jnp.where(good, k + 14 * over14(jnp.maximum(k, 0)) + 14 * c, -1)
    sel[...] = jnp.where(iota((736, ROWS), 1) == target, 1.0, 0.0).astype(BF16)

    loads["w"].wait()
    wsh[...] = jnp.concatenate([wraw[...], jnp.zeros((2, D), BF16)], axis=0)
    loads["hid"].wait()
    pl.semaphore_wait(barrier, len(friends))

    sig = z % 4
    kap = xlo

    def cols(s):
        return pl.ds(pl.multiple_of(((s + 4) % 4) * SLICE, 128), SLICE)

    def wslice(o, s):
        return wbuf.at[c, kap, (y + o + NY) % NY, :, cols(s)]

    def wfull(o, k, core=None):
        return wbuf.at[c if core is None else core, k, (y + o + NY) % NY]

    cross = lax.rem(x + 3 * (1 - xlo) + xlo, NX)
    cross_dev = ((cross % 2) * NZ + z, (y * 2 + cross // 2) * 2 + c)
    send(wsh.at[:, cols(sig)], wx, w0_s, (0,), cross_dev)
    send(hid.at[pl.ds(0, TOK)], hid.at[pl.ds(TOK, TOK)], hid_s, (0,), dev(dc=1))

    loads["lowtb"].wait()
    loads["cot"].wait()
    lane = iota((TOK, 128), 1)
    low_table = lowtb[...]
    for u in range(5):
        tile = jnp.zeros((TOK, 128), F32)
        for i in range(4):
            b = 4 * u + i
            if b < BLOCKS:
                value = dot(cot[:, pl.ds(SPAN * b, SPAN)], low_table)
                tile = jnp.where((lane >= 32 * i) & (lane < 32 * i + 32), value, tile)
        ct[pl.ds(0, TOK), pl.ds(LOW_AT + 128 * u, 128)] = tile.astype(BF16)
    part = pl.ds(LOW_AT, 640)
    send(ct.at[pl.ds(0, TOK), part], ct.at[pl.ds(TOK, TOK), part], ct_s, (4,), dev(dc=1))

    loads["fwd"].wait()
    table = fwd[...]
    for h in range(2):
        high8[h] = dot(cot[:, pl.ds(SPAN * (9 * h + 8), SPAN)], table)
    for s in range(4):
        for q in range(4):
            h, j = q // 2, 4 * (q % 2) + s
            full = dot(cot[:, pl.ds(SPAN * (9 * h + j), SPAN)], table)
            if j < 7:
                extra = high8[h, :, pl.ds(128 * (j // 4), 128)]
                shift = (96 - 32 * (j % 4)) % 128
                extra = pltpu.roll(extra, shift, 1) if shift else extra
            else:
                extra = jnp.zeros((TOK, 128), F32)
            at = 1024 * s + 256 * q
            ct[pl.ds(0, TOK), pl.ds(at, 128)] = full[:, :128].astype(BF16)
            ct[pl.ds(0, TOK), pl.ds(at + 128, 128)] = jnp.where(lane < 96, full[:, 128:], extra).astype(BF16)
        part = pl.ds(1024 * s, 1024)
        send(ct.at[pl.ds(0, TOK), part], ct.at[pl.ds(TOK, TOK), part], ct_s, (s,), dev(dc=1))

    wait(wx, w0_s, (0,))
    own = wsh[:, cols(sig)]
    wslice(0, sig)[...] = jnp.where(jnp.broadcast_to(kap == xhi, own.shape), own, wx[...])

    def wz_send(k):
        for o in FOUND[k]:
            if o:
                wait(wslice(o, sig), wy_s, (slot_of(o),))
            if o in (-2, 2, -3):
                step = 1 if o < 0 else -1
                send(wslice(o, sig), wslice(o, sig), wy_s, (slot_of(o - step),), dev(dy=step))
            send(wslice(o, sig), wslice(o, sig), wza_s, (slot_of(o),), dev(dz=1))
            send(wslice(o, sig), wslice(o, sig), wzb_s, (slot_of(o),), dev(dz=-1))
            if k < NEAR:
                send(wslice(o, sig), wslice(o, sig), wzf_s, (slot_of(o),), dev(dz=2 if o in UP else -2))

    def wz_pass(k):
        for o in FOUND[k]:
            wait(wslice(o, sig - 1), wza_s, (slot_of(o),))
            wait(wslice(o, sig + 1), wzb_s, (slot_of(o),))
            if k < NEAR:
                continue
            if o in UP:
                send(wslice(o, sig - 1), wslice(o, sig - 1), wzf_s, (slot_of(o),), dev(dz=1))
            else:
                send(wslice(o, sig + 1), wslice(o, sig + 1), wzf_s, (slot_of(o),), dev(dz=-1))

    def wx_send(k):
        for o in FOUND[k]:
            wait(wslice(o, sig + 2), wzf_s, (slot_of(o),))
            send(wfull(o, kap), wfull(o, kap), wxx_s, (slot_of(o),), dev(dx=1 if o in UP else -1))
            send(wfull(o, kap), wfull(o, kap), wsib_s, (0, slot_of(o)), dev(dc=1))

    def wx_wait(k):
        for o in FOUND[k]:
            wait(wfull(o, 1 - kap), wxx_s, (slot_of(o),))
            send(wfull(o, 1 - kap), wfull(o, 1 - kap), wsib_s, (1, slot_of(o)), dev(dc=1))

    def wsib_wait(k):
        for o in FOUND[k]:
            wait(wfull(o, kap, 1 - c), wsib_s, (0, slot_of(o)))
            wait(wfull(o, 1 - kap, 1 - c), wsib_s, (1, slot_of(o)))

    for i in (1, -1, 2, -2):
        o = -i
        send(wslice(0, sig), wslice(0, sig), wy_s, (slot_of(o),), dev(dy=i))
    wz_send(0)

    wait(hid.at[pl.ds(TOK, TOK)], hid_s, (0,))
    lhs[...] = dot(sel[...], hid[...], ((1,), (1,))).astype(BF16)
    left = [lhs[pl.ds(256 * i, 256)] for i in range(2)]

    def towards(d, steps):
        return (y + (steps if d == 0 else -steps) + NY) % NY

    def first_hop(s):
        wait(ct.at[pl.ds(TOK, TOK), pl.ds(1024 * s, 1024)], ct_s, (s,))
        for q in range(4):
            gram[pl.ds(256 * q, 256)] = dot(left[q % 2], ct[:, pl.ds(1024 * s + 256 * q, 256)]) * NORM
        for g in range(NY):
            pieces = []
            for pair in range(2):
                a = gram[pl.ds(512 * pair + 32 * g, 32)]
                b = gram[pl.ds(512 * pair + 256 + 32 * g, 32)]
                pieces += [a[:24], a[24:] + b[:8], b[8:]]
            parts[s, g] = jnp.concatenate(pieces, axis=0).astype(BF16)
        for d in range(2):
            send(parts.at[s, towards(d, hops(d, s))], ring.at[d, s, 0], ring_s, (d, s, 0), dev(dy=1 - 2 * d))

    def next_hop(d, s, k):
        wait(ring.at[d, s, k - 1], ring_s, (d, s, k - 1))
        left_over = hops(d, s) - k
        if left_over:
            total = ring[d, s, k - 1].astype(F32) + parts[s, towards(d, left_over)].astype(F32)
            ring[d, s, k - 1] = total.astype(BF16)
            send(ring.at[d, s, k - 1], ring.at[d, s, k], ring_s, (d, s, k), dev(dy=1 - 2 * d))

    for s in range(4):
        first_hop(s)

    m2[...] = jnp.zeros_like(m2)
    loads["mom"].wait()
    for b in range(BLOCKS):
        for h in range(2):
            m2[pl.ds(16 * b, OWN), pl.ds(128 * h, 128)] = mom[pl.ds(2 * b + h, OWN, stride=36), :]
    loads["lowt"].wait()
    lane16 = iota((16, 128), 1)
    kept = dot(m2[...], lowt[...], precision=HI)
    tiles = []
    for u in range(5):
        tile = jnp.zeros((16, 128), F32)
        for i in range(4):
            b = 4 * u + i
            if b < BLOCKS:
                good = (lane16 >= 32 * i) & (lane16 < 32 * i + 32)
                tile = jnp.where(good, 0.9 * kept[16 * b : 16 * b + 16], tile)
        tiles.append(tile)
    spread = jnp.concatenate(tiles, axis=1)
    row, col = iota((HALF, 16), 0), iota((HALF, 16), 1)
    place = jnp.where((row == OWN * (2 * y + xhi) + col) & (col < OWN), 1.0, 0.0).astype(BF16)
    spread_top = spread.astype(BF16)
    placed = dot(place, spread_top) + dot(place, (spread - spread_top.astype(F32)).astype(BF16))
    wait(ct.at[pl.ds(TOK, TOK), pl.ds(LOW_AT, 640)], ct_s, (4,))
    local = dot(lhs[pl.ds(512, HALF)], ct[:, pl.ds(LOW_AT, 640)]) * NORM + placed
    for rt in range(14):
        for u in range(4):
            cbuf[4 * rt + u] = local[16 * rt : 16 * rt + 16, 128 * u : 128 * u + 128].astype(BF16)
    for i in range(7):
        a = local[32 * i : 32 * i + 16, 512:640]
        b = local[32 * i + 16 : 32 * i + 32, 512:640]
        cbuf[56 + i] = jnp.where(lane16 < 64, a, pltpu.roll(b, 64, 1)).astype(BF16)
    cbuf[63] = jnp.zeros((16, 128), BF16)

    def c1_send():
        for i in (1, 3, 2):
            to = (x + i) % NX
            send(cbuf.at[pl.ds(16 * to, 16)], cxr.at[i - 1], c1_s, (i - 1,), dev(dx=i))

    def c2_send():
        total = cbuf[pl.ds(16 * x, 16)].astype(F32)
        for i in (1, 3, 2):
            wait(cxr.at[i - 1], c1_s, (i - 1,))
            total = total + cxr[i - 1].astype(F32)
        cx[...] = total.astype(BF16)
        for i in range(1, NZ):
            send(cx.at[pl.ds(2 * ((z + i) % NZ), 2)], czr.at[i - 1], c2_s, (i - 1,), dev(dz=i))

    def c3_send():
        total = cx[pl.ds(2 * z, 2)].astype(F32)
        for i in range(1, NZ):
            wait(czr.at[i - 1], c2_s, (i - 1,))
            total = total + czr[i - 1].astype(F32)
        cz[...] = total.astype(BF16)
        for i in range(1, NY):
            send(cz, cyr.at[i - 1], c3_s, (i - 1,), dev(dy=i))

    def piece(zz):
        return mbuf.at[c, pl.ds(16 * x + 2 * ((zz + NZ) % NZ), 2)]

    def c4_send():
        total = cz[...].astype(F32)
        for i in range(1, NY):
            wait(cyr.at[i - 1], c3_s, (i - 1,))
            total = total + cyr[i - 1].astype(F32)
        piece(z)[...] = (total * (1.0 / 16.0)).astype(BF16)
        for i in range(1, NZ):
            send(piece(z), piece(z), c4_s, (i - 1,), dev(dz=i))

    def strip(xx, core):
        return mbuf.at[core, pl.ds(16 * ((xx + NX) % NX), 16)]

    def c5_send():
        for i in range(1, NZ):
            wait(piece(z - i), c4_s, (i - 1,))
        for i in (1, 3, 2):
            send(strip(x, c), strip(x, c), c5_s, (i - 1,), dev(dx=i))
        send(strip(x, c), strip(x, c), c6_s, (0,), dev(dc=1))

    def c6_send():
        for i in (1, 3, 2):
            wait(strip(x - i, c), c5_s, (i - 1,))
            send(strip(x - i, c), strip(x - i, c), c6_s, (i,), dev(dc=1))

    def c_done():
        for i in range(NX):
            wait(strip(x - i, 1 - c), c6_s, (i,))

    c1_send()

    row, col = iota((64, 112), 0), iota((64, 112), 1)
    j, q16 = row % 16, row // 16

    def pick_rows(hi):
        return jnp.where((j < OWN) & (col == 28 * q16 + 14 * hi + j), 1.0, 0.0).astype(BF16)

    theirs, ours = pick_rows(1 - xhi), pick_rows(xhi)

    def exchange(s):
        total = parts[s, y].astype(F32)
        for d in range(2):
            total = total + ring[d, s, hops(d, s) - 1].astype(F32)
        chunk = total.astype(BF16)
        xs[s] = dot(theirs, chunk).astype(BF16)
        send(xs.at[s], xr.at[s], x2_s, (s,), dev(dx=2))
        keep[s] = dot(ours, chunk)

    def momentum_rest():
        loads["low"].wait()
        nm2[...] = 0.9 * (m2[...] - dot(kept[:, :KEEP], low[...], precision=HI))

    def left_two():
        loads["acts"].wait()
        a = acts[...]
        for core in range(2):
            i = iota((1, HALF), 1)
            target = i + 14 * over14(i) + 14 * core
            pick = jnp.where(iota((ROWS, HALF), 0) == target, 1.0, 0.0)
            actc[core] = dot(a, pick.astype(BF16)).astype(BF16)
            i = iota((1, 256), 1)
            j, t = i % 16, i // 16
            target = jnp.where(j < OWN, 56 * (t % 8) + 28 * (t // 8) + 14 * core + j, -1)
            pick = jnp.where(iota((ROWS, 256), 0) == target, 1.0, 0.0)
            actw[:, pl.ds(256 * core, 256)] = dot(a, pick.astype(BF16)).astype(BF16)


    events = [
        (8.0, momentum_rest, ()),
        (8.1, left_two, ()),
        (9, wz_pass, (0,)),
        (8.9, wz_send, (1,)),
        (10.1, wz_send, (2,)),
        (11.5, c2_send, ()),
        (11.6, wx_send, (0,)),
        (13.2, wz_send, (3,)),
        (12.3, wz_pass, (1,)),
        (16.4, wz_send, (4,)),
        (13.5, wz_pass, (2,)),
        (12.4, wx_send, (1,)),
        (16, c3_send, ()),
        (16.6, wz_pass, (3,)),
        (19.7, wz_pass, (4,)),
        (17.1, wx_send, (2,)),
        (16, wx_wait, (0,)),
        (20, wx_send, (3,)),
        (18.5, wx_wait, (1,)),
        (20.5, c4_send, ()),
        (23, wx_send, (4,)),
        (22, wx_wait, (2,)),
        (25, c5_send, ()),
        (25.5, wx_wait, (3,)),
        (28, wx_wait, (4,)),
        (29.5, c6_send, ()),
    ]
    at = 12
    for k in range(1, 5):
        for s in range(4):
            for d in range(2):
                if k <= hops(d, s):
                    events.append((at, next_hop, (d, s, k)))
            at += 1.4
    for s in range(4):
        events.append((at + 0.01 * s, exchange, (s,)))
    events.sort(key=lambda event: event[0])
    for _, run, given in events:
        run(*given)

    for k in range(5):
        wsib_wait(k)
    for t in range(4):
        at = pl.ds(SLICE * t, SLICE)
        acc[:, at] = dot(actw[...], wbuf[:, :, :, :, at].reshape(512, SLICE))
    loads["back"].wait()
    inverse = back[...]
    eights = [[jnp.zeros((16, 128), F32) for _ in range(2)] for _ in range(2)]

    def to_space(values):
        big = values.astype(BF16)
        return dot(big, inverse) + dot((values - big.astype(F32)).astype(BF16), inverse)

    for s in range(4):
        wait(xr.at[s], x2_s, (s,))
        total = keep[s] + xr[s].astype(F32)
        space = to_space(total)
        for q in range(4):
            h, j = q // 2, 4 * (q % 2) + s
            at = pl.ds(16 * (9 * h + j), 16)
            nm2[at] = nm2[at] + space[16 * q : 16 * q + 16]
            if j < 7:
                tail = total[16 * q : 16 * q + 16, 128:]
                spot = 32 * (j % 4)
                tail = pltpu.roll(tail, (spot - 96) % 128, 1) if spot != 96 else tail
                good = (lane16 >= spot) & (lane16 < spot + 32)
                eights[h][j // 4] = jnp.where(good, tail, eights[h][j // 4])
    for h in range(2):
        at = pl.ds(16 * (9 * h + 8), 16)
        nm2[at] = nm2[at] + to_space(jnp.concatenate(eights[h], axis=1))

    def kept_part(core, at):
        for rt in range(14):
            for u in range(4):
                call[pl.ds(at + 16 * rt, 16), pl.ds(128 * u, 128)] = mbuf[core, 4 * rt + u]
        for i in range(7):
            tile = mbuf[core, 56 + i].astype(F32)
            call[pl.ds(at + 32 * i, 16), pl.ds(512, 128)] = jnp.where(lane16 < 64, tile, 0.0).astype(BF16)
            call[pl.ds(at + 32 * i + 16, 16), pl.ds(512, 128)] = jnp.where(
                lane16 < 64, pltpu.roll(tile, 64, 1), 0.0
            ).astype(BF16)
        return dot(actc[core], call[pl.ds(at, HALF)])

    inner = kept_part(c, 0)
    c_done()
    inner = inner + kept_part(1 - c, HALF)
    inner = inner * 0.5
    top = inner.astype(BF16)
    rest = (inner - top.astype(F32)).astype(BF16)
    for u in range(5):
        pair_ref[:, pl.ds(256 * u, 128)] = top[:, 128 * u : 128 * u + 128]
        pair_ref[:, pl.ds(256 * u + 128, 128)] = rest[:, 128 * u : 128 * u + 128]

    loads["diag"].wait()
    for copy in pending:
        copy.wait_send()


def finish(acc, pair, nm2, diag, out_h, nm_h, out, nm, sems):
    copies = []
    for u in range(5):
        width = 1024 if u < 4 else 512
        at = pl.ds(1024 * u, width)
        out[:, at] = (acc[:, at] - dot(pair[:, pl.ds(256 * u, 256)], diag[:, pl.ds(0, width)])).astype(BF16)
        copies.append(pltpu.make_async_copy(out.at[:, at], out_h.at[:, at], sems.at[u]))
        copies[-1].start()
    for b in range(BLOCKS):
        for h in range(2):
            nm[pl.ds(2 * b + h, OWN, stride=36), :] = nm2[pl.ds(16 * b, OWN), pl.ds(128 * h, 128)]
    copies.append(pltpu.make_async_copy(nm, nm_h, sems.at[5]))
    copies[-1].start()
    for copy in copies:
        copy.wait()


def local(hid_acts, out_cot, momentum, weight, next_acts):
    any_space = pl.BlockSpec(memory_space=pl.ANY)
    hbm = pl.BlockSpec(memory_space=pltpu.HBM)
    vmem = pl.BlockSpec(memory_space=pltpu.VMEM)
    dma = pltpu.SemaphoreType.DMA
    scratch = [
        pltpu.VMEM((TOK, D), BF16),
        pltpu.VMEM((2 * TOK, ROWS), BF16),
        pltpu.VMEM((TOK, ROWS), BF16),
        pltpu.VMEM((504, 128), F32),
        pltpu.VMEM((OWN, D), BF16),
        pltpu.VMEM((SPAN, SPAN), BF16),
        pltpu.VMEM((SPAN, SPAN), BF16),
        pltpu.VMEM((SPAN, 128), F32),
        pltpu.VMEM((SPAN, 128), BF16),
        pltpu.VMEM((KEEP, SPAN), F32),
        pltpu.VMEM((2 * TOK, CT), BF16),
        pltpu.VMEM((736, ROWS), BF16),
        pltpu.VMEM((736, 2 * TOK), BF16),
        pltpu.VMEM((1024, 256), F32),
        pltpu.VMEM((4, NY, 112, 256), BF16),
        pltpu.VMEM((2, 4, 4, 112, 256), BF16),
        pltpu.VMEM((4, 64, 256), BF16),
        pltpu.VMEM((4, 64, 256), BF16),
        pltpu.VMEM((4, 64, 256), F32),
        pltpu.VMEM((16 * BLOCKS, SPAN), F32),
        pltpu.VMEM((2, TOK, SPAN), F32),
        pltpu.VMEM((16, D), BF16),
        pltpu.VMEM((16, SLICE), BF16),
        pltpu.VMEM((2, 2, NY, 16, D), BF16),
        pltpu.VMEM((64, 16, 128), BF16),
        pltpu.VMEM((3, 16, 16, 128), BF16),
        pltpu.VMEM((16, 16, 128), BF16),
        pltpu.VMEM((7, 2, 16, 128), BF16),
        pltpu.VMEM((2, 16, 128), BF16),
        pltpu.VMEM((7, 2, 16, 128), BF16),
        pltpu.VMEM((2, 64, 16, 128), BF16),
        pltpu.VMEM((ROWS, 640), BF16),
        pltpu.VMEM((TOK, 512), BF16),
        pltpu.VMEM((2, TOK, HALF), BF16),
        dma((11,)),
        dma((2, 1)),
        dma((2, 5)),
        dma((2, 2, 4, 4)),
        dma((2, 4)),
        dma((2, 1)),
        dma((2, 8)),
        dma((2, 8)),
        dma((2, 8)),
        dma((2, 8)),
        dma((2, 8)),
        dma((2, 2, 8)),
        dma((2, 3)),
        dma((2, 7)),
        dma((2, 7)),
        dma((2, 7)),
        dma((2, 3)),
        dma((2, 4)),
    ]
    given = (
        hid_acts,
        out_cot,
        momentum.reshape(504, 128),
        weight.reshape(OWN, D),
        next_acts,
        *tables(),
    )
    held = pl.pallas_call(
        kernel,
        out_shape=(
            pltpu.VMEM((TOK, D), F32),
            pltpu.VMEM((TOK, 5 * SPAN), BF16),
            pltpu.VMEM((16 * BLOCKS, SPAN), F32),
            pltpu.VMEM((SPAN, 1024), BF16),
        ),
        in_specs=[hbm] * 11,
        out_specs=(vmem,) * 4,
        scratch_shapes=scratch,
        compiler_params=pltpu.CompilerParams(
            collective_id=0, has_side_effects=True, vmem_limit_bytes=40 * 2**20
        ),
        name="step",
    )(
        *(pltpu.with_memory_space_constraint(a, pltpu.HBM) for a in given)
    )
    held = [pltpu.with_memory_space_constraint(a, pltpu.VMEM) for a in held]
    out, nm = pl.pallas_call(
        finish,
        out_shape=(
            jax.ShapeDtypeStruct((TOK, D), BF16),
            jax.ShapeDtypeStruct((504, 128), F32),
        ),
        in_specs=[vmem] * 4,
        out_specs=(any_space, any_space),
        scratch_shapes=[pltpu.VMEM((TOK, D), BF16), pltpu.VMEM((504, 128), F32), dma((6,))],
        compiler_params=pltpu.CompilerParams(vmem_limit_bytes=8 * 2**20),
        name="finish",
    )(*held)
    return out[None], nm.reshape(1, OWN, 1, D)


def solution(mesh):
    return jax.shard_map(
        local,
        mesh=mesh,
        in_specs=(
            P(None, ("rep", "fsdp"), None),
            P(None, ("rep", "fsdp"), None),
            P("rep", "fsdp", None, None),
            P("fsdp", None, None),
            P(None, ("rep", "fsdp"), None),
        ),
        out_specs=(P(None, ("rep", "fsdp"), None), P("rep", "fsdp", None, None)),
        check_vma=False,
    )
```

```python
import math

import jax
import jax.numpy as jnp
import numpy as np
from jax import lax
from jax.experimental import pallas as pl
from jax.experimental.pallas import tpu as pltpu
from jax.sharding import PartitionSpec as P

SPAN = 256
KEEP = 32
HIGH = SPAN - KEEP
TOK = 192
ROWS = 448
D = 4608
BLOCKS = D // SPAN
OWN = 14
HALF = 224
NY, NZ, NX = 8, 8, 4
SLICE = D // 4
LOW_AT = 4096
CT = LOW_AT + 640
NORM = 1.0 / math.sqrt(TOK * 32)
F32, BF16 = jnp.float32, jnp.bfloat16
HI = lax.Precision.HIGHEST


def tables():
    k = np.arange(SPAN, dtype=np.float64)[:, None]
    n = np.arange(SPAN, dtype=np.float64)[None, :]
    dct = np.cos(np.pi * (2.0 * n + 1.0) * k / (2.0 * SPAN)) * np.sqrt(2.0 / SPAN)
    dct[0] *= np.sqrt(0.5)
    low, high = dct[:KEEP], dct[KEEP:]
    forward = np.concatenate([high, low], axis=0).T
    back = np.concatenate([high, np.zeros((KEEP, SPAN))], axis=0)
    low_t = np.tile(low.T, (1, 4))
    diag = np.zeros((128, 1024))
    for i in range(4):
        diag[32 * i : 32 * i + 32, 256 * i : 256 * i + 256] = low
    diag = np.concatenate([diag, diag], axis=0)
    return (
        jnp.asarray(forward, BF16),
        jnp.asarray(back, BF16),
        jnp.asarray(low_t, F32),
        jnp.asarray(low_t, BF16),
        jnp.asarray(low, F32),
        jnp.asarray(diag, BF16),
    )


def dot(a, b, contract=((1,), (0,)), precision=None):
    return lax.dot_general(
        a, b, (contract, ((), ())), precision=precision, preferred_element_type=F32
    )


def iota(shape, dim):
    return lax.broadcasted_iota(jnp.int32, shape, dim)


def over14(i):
    return (i * 4682) >> 16


FOUND = ((0,), (-1, 1), (-2, 2), (-3, 3), (-4,))
UP = (0, -1, -2, -3)
NEAR = 2


def slot_of(o):
    return o + 4


def hops(d, s):
    return 4 if (s < 2) == (d == 0) else 3


def kernel(
    hid_h, cot_h, mom_h, w_h, act_h, fwd_h, back_h, lowt_h, lowtb_h, low_h, diag_h,
    acc, pair_ref, nm2, diag,
    cot, hid, acts, mom, wraw, fwd, back, lowt, lowtb, low,
    ct, sel, lhs, gram, parts, ring, xs, xr, keep, m2, high8,
    wsh, wx, wbuf, cbuf, cxr, cx, czr, cz, cyr, mbuf, call, actw, actc,
    lsem, hid_s, ct_s, ring_s, x2_s, w0_s, wy_s, wza_s, wzb_s, wzf_s, wxx_s, wsib_s,
    c1_s, c2_s, c3_s, c4_s, c5_s, c6_s,
):
    rep, f = lax.axis_index("rep"), lax.axis_index("fsdp")
    xlo, z = rep // NZ, rep % NZ
    y, xhi, c = f // 4, (f // 2) % 2, f % 2
    x = xhi * 2 + xlo

    def dev(dx=0, dy=0, dz=0, dc=0):
        xx, yy, zz, cc = (x + dx + NX) % NX, (y + dy + NY) % NY, (z + dz + NZ) % NZ, (c + dc) % 2
        return ((xx % 2) * NZ + zz, (yy * 2 + xx // 2) * 2 + cc)

    pending = []

    def send(src, dst, sems, index, to):
        copy = pltpu.make_async_remote_copy(
            src_ref=src, dst_ref=dst, send_sem=sems.at[(0,) + index], recv_sem=sems.at[(1,) + index],
            device_id=to, device_id_type=pl.DeviceIdType.MESH,
        )
        copy.start()
        pending.append(copy)

    def wait(dst, sems, index):
        pltpu.make_async_remote_copy(
            src_ref=dst, dst_ref=dst, send_sem=sems.at[(0,) + index], recv_sem=sems.at[(1,) + index],
            device_id=dev(dc=1), device_id_type=pl.DeviceIdType.MESH,
        ).wait_recv()

    loads = {}
    for i, (name, src, dst) in enumerate((
        ("w", w_h, wraw), ("hid", hid_h.at[0], hid.at[pl.ds(0, TOK)]), ("lowtb", lowtb_h, lowtb),
        ("cot", cot_h.at[0], cot), ("fwd", fwd_h, fwd), ("mom", mom_h, mom), ("lowt", lowt_h, lowt),
        ("low", low_h, low), ("acts", act_h.at[0], acts), ("back", back_h, back), ("diag", diag_h, diag),
    )):
        loads[name] = pltpu.make_async_copy(src, dst, lsem.at[i])
        loads[name].start()

    barrier = pltpu.get_barrier_semaphore()
    friends = [dev(dc=1)]
    friends += [dev(dx=i) for i in range(1, NX)]
    friends += [dev(dy=i) for i in range(1, NY)]
    friends += [dev(dz=i) for i in range(1, NZ)]
    for friend in friends:
        pl.semaphore_signal(barrier, inc=1, device_id=friend, device_id_type=pl.DeviceIdType.MESH)

    i = iota((736, 1), 0)
    w = jnp.where(i < 256, i % 32, i % 32 - 4)
    k = jnp.where(i < 512, 28 * ((i % 256) // 32) + w, i - 512)
    good = (i >= 512) | ((w >= 0) & (w < 28))
    target = jnp.where(good, k + 14 * over14(jnp.maximum(k, 0)) + 14 * c, -1)
    sel[...] = jnp.where(iota((736, ROWS), 1) == target, 1.0, 0.0).astype(BF16)

    loads["w"].wait()
    wsh[...] = jnp.concatenate([wraw[...], jnp.zeros((2, D), BF16)], axis=0)
    loads["hid"].wait()
    pl.semaphore_wait(barrier, len(friends))

    sig = z % 4
    kap = xlo

    def cols(s):
        return pl.ds(pl.multiple_of(((s + 4) % 4) * SLICE, 128), SLICE)

    def wslice(o, s):
        return wbuf.at[c, kap, (y + o + NY) % NY, :, cols(s)]

    def wfull(o, k, core=None):
        return wbuf.at[c if core is None else core, k, (y + o + NY) % NY]

    cross = lax.rem(x + 3 * (1 - xlo) + xlo, NX)
    cross_dev = ((cross % 2) * NZ + z, (y * 2 + cross // 2) * 2 + c)
    send(wsh.at[:, cols(sig)], wx, w0_s, (0,), cross_dev)
    send(hid.at[pl.ds(0, TOK)], hid.at[pl.ds(TOK, TOK)], hid_s, (0,), dev(dc=1))

    loads["lowtb"].wait()
    loads["cot"].wait()
    lane = iota((TOK, 128), 1)
    low_table = lowtb[...]
    for u in range(5):
        tile = jnp.zeros((TOK, 128), F32)
        for i in range(4):
            b = 4 * u + i
            if b < BLOCKS:
                value = dot(cot[:, pl.ds(SPAN * b, SPAN)], low_table)
                tile = jnp.where((lane >= 32 * i) & (lane < 32 * i + 32), value, tile)
        ct[pl.ds(0, TOK), pl.ds(LOW_AT + 128 * u, 128)] = tile.astype(BF16)
    part = pl.ds(LOW_AT, 640)
    send(ct.at[pl.ds(0, TOK), part], ct.at[pl.ds(TOK, TOK), part], ct_s, (4,), dev(dc=1))

    loads["fwd"].wait()
    table = fwd[...]
    for h in range(2):
        high8[h] = dot(cot[:, pl.ds(SPAN * (9 * h + 8), SPAN)], table)
    for s in range(4):
        for q in range(4):
            h, j = q // 2, 4 * (q % 2) + s
            full = dot(cot[:, pl.ds(SPAN * (9 * h + j), SPAN)], table)
            if j < 7:
                extra = high8[h, :, pl.ds(128 * (j // 4), 128)]
                shift = (96 - 32 * (j % 4)) % 128
                extra = pltpu.roll(extra, shift, 1) if shift else extra
            else:
                extra = jnp.zeros((TOK, 128), F32)
            at = 1024 * s + 256 * q
            ct[pl.ds(0, TOK), pl.ds(at, 128)] = full[:, :128].astype(BF16)
            ct[pl.ds(0, TOK), pl.ds(at + 128, 128)] = jnp.where(lane < 96, full[:, 128:], extra).astype(BF16)
        part = pl.ds(1024 * s, 1024)
        send(ct.at[pl.ds(0, TOK), part], ct.at[pl.ds(TOK, TOK), part], ct_s, (s,), dev(dc=1))

    m2[...] = jnp.zeros_like(m2)
    loads["mom"].wait()
    for b in range(BLOCKS):
        for h in range(2):
            m2[pl.ds(16 * b, OWN), pl.ds(128 * h, 128)] = mom[pl.ds(2 * b + h, OWN, stride=36), :]
    loads["lowt"].wait()
    lane16 = iota((16, 128), 1)
    kept = dot(m2[...], lowt[...], precision=HI)
    tiles = []
    for u in range(5):
        tile = jnp.zeros((16, 128), F32)
        for i in range(4):
            b = 4 * u + i
            if b < BLOCKS:
                good = (lane16 >= 32 * i) & (lane16 < 32 * i + 32)
                tile = jnp.where(good, 0.9 * kept[16 * b : 16 * b + 16], tile)
        tiles.append(tile)
    spread = jnp.concatenate(tiles, axis=1)
    row, col = iota((HALF, 16), 0), iota((HALF, 16), 1)
    place = jnp.where((row == OWN * (2 * y + xhi) + col) & (col < OWN), 1.0, 0.0).astype(BF16)
    spread_top = spread.astype(BF16)
    placed = dot(place, spread_top) + dot(place, (spread - spread_top.astype(F32)).astype(BF16))

    wait(wx, w0_s, (0,))
    own = wsh[:, cols(sig)]
    wslice(0, sig)[...] = jnp.where(jnp.broadcast_to(kap == xhi, own.shape), own, wx[...])

    def wz_send(k):
        for o in FOUND[k]:
            if o:
                wait(wslice(o, sig), wy_s, (slot_of(o),))
            if o in (-2, 2, -3):
                step = 1 if o < 0 else -1
                send(wslice(o, sig), wslice(o, sig), wy_s, (slot_of(o - step),), dev(dy=step))
            send(wslice(o, sig), wslice(o, sig), wza_s, (slot_of(o),), dev(dz=1))
            send(wslice(o, sig), wslice(o, sig), wzb_s, (slot_of(o),), dev(dz=-1))
            if k < NEAR:
                send(wslice(o, sig), wslice(o, sig), wzf_s, (slot_of(o),), dev(dz=2 if o in UP else -2))

    def wz_pass(k):
        for o in FOUND[k]:
            wait(wslice(o, sig - 1), wza_s, (slot_of(o),))
            wait(wslice(o, sig + 1), wzb_s, (slot_of(o),))
            if k < NEAR:
                continue
            if o in UP:
                send(wslice(o, sig - 1), wslice(o, sig - 1), wzf_s, (slot_of(o),), dev(dz=1))
            else:
                send(wslice(o, sig + 1), wslice(o, sig + 1), wzf_s, (slot_of(o),), dev(dz=-1))

    def wx_send(k):
        for o in FOUND[k]:
            wait(wslice(o, sig + 2), wzf_s, (slot_of(o),))
            send(wfull(o, kap), wfull(o, kap), wxx_s, (slot_of(o),), dev(dx=1 if o in UP else -1))
            send(wfull(o, kap), wfull(o, kap), wsib_s, (0, slot_of(o)), dev(dc=1))

    def wx_wait(k):
        for o in FOUND[k]:
            wait(wfull(o, 1 - kap), wxx_s, (slot_of(o),))
            send(wfull(o, 1 - kap), wfull(o, 1 - kap), wsib_s, (1, slot_of(o)), dev(dc=1))

    def wsib_wait(k):
        for o in FOUND[k]:
            wait(wfull(o, kap, 1 - c), wsib_s, (0, slot_of(o)))
            wait(wfull(o, 1 - kap, 1 - c), wsib_s, (1, slot_of(o)))

    for i in (1, -1, 2, -2):
        o = -i
        send(wslice(0, sig), wslice(0, sig), wy_s, (slot_of(o),), dev(dy=i))
    wz_send(0)

    wait(hid.at[pl.ds(TOK, TOK)], hid_s, (0,))
    lhs[...] = dot(sel[...], hid[...], ((1,), (1,))).astype(BF16)
    left = [lhs[pl.ds(256 * i, 256)] for i in range(2)]

    def towards(d, steps):
        return (y + (steps if d == 0 else -steps) + NY) % NY

    def first_hop(s):
        wait(ct.at[pl.ds(TOK, TOK), pl.ds(1024 * s, 1024)], ct_s, (s,))
        for q in range(4):
            gram[pl.ds(256 * q, 256)] = dot(left[q % 2], ct[:, pl.ds(1024 * s + 256 * q, 256)]) * NORM
        for g in range(NY):
            pieces = []
            for pair in range(2):
                a = gram[pl.ds(512 * pair + 32 * g, 32)]
                b = gram[pl.ds(512 * pair + 256 + 32 * g, 32)]
                pieces += [a[:24], a[24:] + b[:8], b[8:]]
            parts[s, g] = jnp.concatenate(pieces, axis=0).astype(BF16)
        for d in range(2):
            send(parts.at[s, towards(d, hops(d, s))], ring.at[d, s, 0], ring_s, (d, s, 0), dev(dy=1 - 2 * d))

    def next_hop(d, s, k):
        wait(ring.at[d, s, k - 1], ring_s, (d, s, k - 1))
        left_over = hops(d, s) - k
        if left_over:
            total = ring[d, s, k - 1].astype(F32) + parts[s, towards(d, left_over)].astype(F32)
            ring[d, s, k - 1] = total.astype(BF16)
            send(ring.at[d, s, k - 1], ring.at[d, s, k], ring_s, (d, s, k), dev(dy=1 - 2 * d))

    for s in range(4):
        first_hop(s)

    wait(ct.at[pl.ds(TOK, TOK), pl.ds(LOW_AT, 640)], ct_s, (4,))
    local = dot(lhs[pl.ds(512, HALF)], ct[:, pl.ds(LOW_AT, 640)]) * NORM + placed
    for rt in range(14):
        for u in range(4):
            cbuf[4 * rt + u] = local[16 * rt : 16 * rt + 16, 128 * u : 128 * u + 128].astype(BF16)
    for i in range(7):
        a = local[32 * i : 32 * i + 16, 512:640]
        b = local[32 * i + 16 : 32 * i + 32, 512:640]
        cbuf[56 + i] = jnp.where(lane16 < 64, a, pltpu.roll(b, 64, 1)).astype(BF16)
    cbuf[63] = jnp.zeros((16, 128), BF16)

    def c1_send():
        for i in (1, 3, 2):
            to = (x + i) % NX
            send(cbuf.at[pl.ds(16 * to, 16)], cxr.at[i - 1], c1_s, (i - 1,), dev(dx=i))

    def c2_send():
        total = cbuf[pl.ds(16 * x, 16)].astype(F32)
        for i in (1, 3, 2):
            wait(cxr.at[i - 1], c1_s, (i - 1,))
            total = total + cxr[i - 1].astype(F32)
        cx[...] = total.astype(BF16)
        for i in range(1, NZ):
            send(cx.at[pl.ds(2 * ((z + i) % NZ), 2)], czr.at[i - 1], c2_s, (i - 1,), dev(dz=i))

    def c3_send():
        total = cx[pl.ds(2 * z, 2)].astype(F32)
        for i in range(1, NZ):
            wait(czr.at[i - 1], c2_s, (i - 1,))
            total = total + czr[i - 1].astype(F32)
        cz[...] = total.astype(BF16)
        for i in range(1, NY):
            send(cz, cyr.at[i - 1], c3_s, (i - 1,), dev(dy=i))

    def piece(zz):
        return mbuf.at[c, pl.ds(16 * x + 2 * ((zz + NZ) % NZ), 2)]

    def c4_send():
        total = cz[...].astype(F32)
        for i in range(1, NY):
            wait(cyr.at[i - 1], c3_s, (i - 1,))
            total = total + cyr[i - 1].astype(F32)
        piece(z)[...] = (total * (1.0 / 16.0)).astype(BF16)
        for i in range(1, NZ):
            send(piece(z), piece(z), c4_s, (i - 1,), dev(dz=i))

    def strip(xx, core):
        return mbuf.at[core, pl.ds(16 * ((xx + NX) % NX), 16)]

    def c5_send():
        for i in range(1, NZ):
            wait(piece(z - i), c4_s, (i - 1,))
        for i in (1, 3, 2):
            send(strip(x, c), strip(x, c), c5_s, (i - 1,), dev(dx=i))
        send(strip(x, c), strip(x, c), c6_s, (0,), dev(dc=1))

    def c6_send():
        for i in (1, 3, 2):
            wait(strip(x - i, c), c5_s, (i - 1,))
            send(strip(x - i, c), strip(x - i, c), c6_s, (i,), dev(dc=1))

    def c_done():
        for i in range(NX):
            wait(strip(x - i, 1 - c), c6_s, (i,))

    c1_send()

    row, col = iota((64, 112), 0), iota((64, 112), 1)
    j, q16 = row % 16, row // 16

    def pick_rows(hi):
        return jnp.where((j < OWN) & (col == 28 * q16 + 14 * hi + j), 1.0, 0.0).astype(BF16)

    theirs, ours = pick_rows(1 - xhi), pick_rows(xhi)

    def exchange(s):
        total = parts[s, y].astype(F32)
        for d in range(2):
            total = total + ring[d, s, hops(d, s) - 1].astype(F32)
        chunk = total.astype(BF16)
        xs[s] = dot(theirs, chunk).astype(BF16)
        send(xs.at[s], xr.at[s], x2_s, (s,), dev(dx=2))
        keep[s] = dot(ours, chunk)

    def momentum_rest():
        loads["low"].wait()
        nm2[...] = 0.9 * (m2[...] - dot(kept[:, :KEEP], low[...], precision=HI))

    def left_two():
        loads["acts"].wait()
        a = acts[...]
        for core in range(2):
            i = iota((1, HALF), 1)
            target = i + 14 * over14(i) + 14 * core
            pick = jnp.where(iota((ROWS, HALF), 0) == target, 1.0, 0.0)
            actc[core] = dot(a, pick.astype(BF16)).astype(BF16)
            i = iota((1, 256), 1)
            j, t = i % 16, i // 16
            target = jnp.where(j < OWN, 56 * (t % 8) + 28 * (t // 8) + 14 * core + j, -1)
            pick = jnp.where(iota((ROWS, 256), 0) == target, 1.0, 0.0)
            actw[:, pl.ds(256 * core, 256)] = dot(a, pick.astype(BF16)).astype(BF16)


    events = [
        (8.0, momentum_rest, ()),
        (8.1, left_two, ()),
        (9, wz_pass, (0,)),
        (8.9, wz_send, (1,)),
        (10.1, wz_send, (2,)),
        (11.5, c2_send, ()),
        (11.6, wx_send, (0,)),
        (13.2, wz_send, (3,)),
        (12.3, wz_pass, (1,)),
        (16.4, wz_send, (4,)),
        (13.5, wz_pass, (2,)),
        (12.4, wx_send, (1,)),
        (16, c3_send, ()),
        (16.6, wz_pass, (3,)),
        (19.7, wz_pass, (4,)),
        (17.1, wx_send, (2,)),
        (16, wx_wait, (0,)),
        (20, wx_send, (3,)),
        (18.5, wx_wait, (1,)),
        (20.5, c4_send, ()),
        (23, wx_send, (4,)),
        (22, wx_wait, (2,)),
        (25, c5_send, ()),
        (25.5, wx_wait, (3,)),
        (28, wx_wait, (4,)),
        (29.5, c6_send, ()),
    ]
    at = 12
    for k in range(1, 5):
        for s in range(4):
            for d in range(2):
                if k <= hops(d, s):
                    events.append((at, next_hop, (d, s, k)))
            at += 1.4
    for s in range(4):
        events.append((at + 0.01 * s, exchange, (s,)))
    events.sort(key=lambda event: event[0])
    for _, run, given in events:
        run(*given)

    for k in range(5):
        wsib_wait(k)
    for t in range(4):
        at = pl.ds(SLICE * t, SLICE)
        acc[:, at] = dot(actw[...], wbuf[:, :, :, :, at].reshape(512, SLICE))
    loads["back"].wait()
    inverse = back[...]
    eights = [[jnp.zeros((16, 128), F32) for _ in range(2)] for _ in range(2)]

    def to_space(values):
        big = values.astype(BF16)
        return dot(big, inverse) + dot((values - big.astype(F32)).astype(BF16), inverse)

    for s in range(4):
        wait(xr.at[s], x2_s, (s,))
        total = keep[s] + xr[s].astype(F32)
        space = to_space(total)
        for q in range(4):
            h, j = q // 2, 4 * (q % 2) + s
            at = pl.ds(16 * (9 * h + j), 16)
            nm2[at] = nm2[at] + space[16 * q : 16 * q + 16]
            if j < 7:
                tail = total[16 * q : 16 * q + 16, 128:]
                spot = 32 * (j % 4)
                tail = pltpu.roll(tail, (spot - 96) % 128, 1) if spot != 96 else tail
                good = (lane16 >= spot) & (lane16 < spot + 32)
                eights[h][j // 4] = jnp.where(good, tail, eights[h][j // 4])
    for h in range(2):
        at = pl.ds(16 * (9 * h + 8), 16)
        nm2[at] = nm2[at] + to_space(jnp.concatenate(eights[h], axis=1))

    def kept_part(core, at):
        for rt in range(14):
            for u in range(4):
                call[pl.ds(at + 16 * rt, 16), pl.ds(128 * u, 128)] = mbuf[core, 4 * rt + u]
        for i in range(7):
            tile = mbuf[core, 56 + i].astype(F32)
            call[pl.ds(at + 32 * i, 16), pl.ds(512, 128)] = jnp.where(lane16 < 64, tile, 0.0).astype(BF16)
            call[pl.ds(at + 32 * i + 16, 16), pl.ds(512, 128)] = jnp.where(
                lane16 < 64, pltpu.roll(tile, 64, 1), 0.0
            ).astype(BF16)
        return dot(actc[core], call[pl.ds(at, HALF)])

    inner = kept_part(c, 0)
    c_done()
    inner = inner + kept_part(1 - c, HALF)
    inner = inner * 0.5
    top = inner.astype(BF16)
    rest = (inner - top.astype(F32)).astype(BF16)
    for u in range(5):
        pair_ref[:, pl.ds(256 * u, 128)] = top[:, 128 * u : 128 * u + 128]
        pair_ref[:, pl.ds(256 * u + 128, 128)] = rest[:, 128 * u : 128 * u + 128]

    loads["diag"].wait()
    for copy in pending:
        copy.wait_send()


def finish(acc, pair, nm2, diag, out_h, nm_h, out, nm, sems):
    copies = []
    for u in range(5):
        width = 1024 if u < 4 else 512
        at = pl.ds(1024 * u, width)
        out[:, at] = (acc[:, at] - dot(pair[:, pl.ds(256 * u, 256)], diag[:, pl.ds(0, width)])).astype(BF16)
        copies.append(pltpu.make_async_copy(out.at[:, at], out_h.at[:, at], sems.at[u]))
        copies[-1].start()
    for b in range(BLOCKS):
        for h in range(2):
            nm[pl.ds(2 * b + h, OWN, stride=36), :] = nm2[pl.ds(16 * b, OWN), pl.ds(128 * h, 128)]
    copies.append(pltpu.make_async_copy(nm, nm_h, sems.at[5]))
    copies[-1].start()
    for copy in copies:
        copy.wait()


def local(hid_acts, out_cot, momentum, weight, next_acts):
    any_space = pl.BlockSpec(memory_space=pl.ANY)
    hbm = pl.BlockSpec(memory_space=pltpu.HBM)
    vmem = pl.BlockSpec(memory_space=pltpu.VMEM)
    dma = pltpu.SemaphoreType.DMA
    scratch = [
        pltpu.VMEM((TOK, D), BF16),
        pltpu.VMEM((2 * TOK, ROWS), BF16),
        pltpu.VMEM((TOK, ROWS), BF16),
        pltpu.VMEM((504, 128), F32),
        pltpu.VMEM((OWN, D), BF16),
        pltpu.VMEM((SPAN, SPAN), BF16),
        pltpu.VMEM((SPAN, SPAN), BF16),
        pltpu.VMEM((SPAN, 128), F32),
        pltpu.VMEM((SPAN, 128), BF16),
        pltpu.VMEM((KEEP, SPAN), F32),
        pltpu.VMEM((2 * TOK, CT), BF16),
        pltpu.VMEM((736, ROWS), BF16),
        pltpu.VMEM((736, 2 * TOK), BF16),
        pltpu.VMEM((1024, 256), F32),
        pltpu.VMEM((4, NY, 112, 256), BF16),
        pltpu.VMEM((2, 4, 4, 112, 256), BF16),
        pltpu.VMEM((4, 64, 256), BF16),
        pltpu.VMEM((4, 64, 256), BF16),
        pltpu.VMEM((4, 64, 256), F32),
        pltpu.VMEM((16 * BLOCKS, SPAN), F32),
        pltpu.VMEM((2, TOK, SPAN), F32),
        pltpu.VMEM((16, D), BF16),
        pltpu.VMEM((16, SLICE), BF16),
        pltpu.VMEM((2, 2, NY, 16, D), BF16),
        pltpu.VMEM((64, 16, 128), BF16),
        pltpu.VMEM((3, 16, 16, 128), BF16),
        pltpu.VMEM((16, 16, 128), BF16),
        pltpu.VMEM((7, 2, 16, 128), BF16),
        pltpu.VMEM((2, 16, 128), BF16),
        pltpu.VMEM((7, 2, 16, 128), BF16),
        pltpu.VMEM((2, 64, 16, 128), BF16),
        pltpu.VMEM((ROWS, 640), BF16),
        pltpu.VMEM((TOK, 512), BF16),
        pltpu.VMEM((2, TOK, HALF), BF16),
        dma((11,)),
        dma((2, 1)),
        dma((2, 5)),
        dma((2, 2, 4, 4)),
        dma((2, 4)),
        dma((2, 1)),
        dma((2, 8)),
        dma((2, 8)),
        dma((2, 8)),
        dma((2, 8)),
        dma((2, 8)),
        dma((2, 2, 8)),
        dma((2, 3)),
        dma((2, 7)),
        dma((2, 7)),
        dma((2, 7)),
        dma((2, 3)),
        dma((2, 4)),
    ]
    given = (
        hid_acts,
        out_cot,
        momentum.reshape(504, 128),
        weight.reshape(OWN, D),
        next_acts,
        *tables(),
    )
    held = pl.pallas_call(
        kernel,
        out_shape=(
            pltpu.VMEM((TOK, D), F32),
            pltpu.VMEM((TOK, 5 * SPAN), BF16),
            pltpu.VMEM((16 * BLOCKS, SPAN), F32),
            pltpu.VMEM((SPAN, 1024), BF16),
        ),
        in_specs=[hbm] * 11,
        out_specs=(vmem,) * 4,
        scratch_shapes=scratch,
        compiler_params=pltpu.CompilerParams(
            collective_id=0, has_side_effects=True, vmem_limit_bytes=40 * 2**20
        ),
        name="step",
    )(
        *(pltpu.with_memory_space_constraint(a, pltpu.HBM) for a in given)
    )
    held = [pltpu.with_memory_space_constraint(a, pltpu.VMEM) for a in held]
    out, nm = pl.pallas_call(
        finish,
        out_shape=(
            jax.ShapeDtypeStruct((TOK, D), BF16),
            jax.ShapeDtypeStruct((504, 128), F32),
        ),
        in_specs=[vmem] * 4,
        out_specs=(any_space, any_space),
        scratch_shapes=[pltpu.VMEM((TOK, D), BF16), pltpu.VMEM((504, 128), F32), dma((6,))],
        compiler_params=pltpu.CompilerParams(vmem_limit_bytes=8 * 2**20),
        name="finish",
    )(*held)
    return out[None], nm.reshape(1, OWN, 1, D)


def solution(mesh):
    return jax.shard_map(
        local,
        mesh=mesh,
        in_specs=(
            P(None, ("rep", "fsdp"), None),
            P(None, ("rep", "fsdp"), None),
            P("rep", "fsdp", None, None),
            P("fsdp", None, None),
            P(None, ("rep", "fsdp"), None),
        ),
        out_specs=(P(None, ("rep", "fsdp"), None), P("rep", "fsdp", None, None)),
        check_vma=False,
    )
```
